512 devices in a mesh: code: 128 (over y, z, core), tok: 4 (over x).
Axes of the slice: x: 4, y: 8, z: 8, core: 2. Of those that a mesh axis runs over, the one named last changes fastest.
Arguments:
- tokens: bfloat16 [4096, 256], P('tok'), may hold values from -125 to 125
- codebook: bfloat16 [262144, 256], P('code'), may hold values from -2 to 2
- cotangent: bfloat16 [4096, 256], P('tok'), may hold values from -6 to 6
- indices: int32 [4096], P('tok'), may hold values from 0 to 262143
Outputs:
- grad_tokens: float32 [4096, 256], P('tok')
- grad_codebook: float32 [262144, 256], P(('code', 'tok'))
The draws below stay inside these ranges and needn't reach their ends.
All inputs are finite; a program needn't handle non-finite values.
Results may differ from the reference program's by a relative error of at most 0.0095.
Values may be sent and summed in bfloat16 or wider, within the bound.
A program may use at most 64 MiB of HBM per device.

```python
import jax
import jax.numpy as jnp
from jax import lax

D = 256
CODE_DEV = 2048
TOK_DEV = 1024
CODES = 262144
TOKENS = 4096
N_TOK = 4


def shared_codes(key):
    base = 0.1875 * jnp.clip(jax.random.normal(key, (CODES, D), jnp.float32), -6.0, 6.0)
    return base


def draw_codebook(key, part):
    base = shared_codes(key)
    return base.astype(jnp.bfloat16)


def draw_tokens(key, part):
    key = jax.random.fold_in(key, 2)
    latent = jnp.clip(jax.random.normal(key, (TOKENS, D), jnp.float32), -6.0, 6.0)
    return latent.astype(jnp.bfloat16)


def set_ends(values, stream_key, least, high):
    spot = [jax.random.randint(jax.random.fold_in(stream_key, axis), (), 0, length) for axis, length in enumerate(values.shape)]
    widest = values.shape.index(max(values.shape))
    next_to = spot[:widest] + [(spot[widest] + 1) % values.shape[widest]] + spot[widest + 1:]
    return values.at[tuple(spot)].set(least).at[tuple(next_to)].set(high)


def block_scale(stream_key, extent, split, least, top_value):
    gain = 1.0
    for position, blocks in split:
        heights = jax.random.uniform(jax.random.fold_in(jax.random.fold_in(stream_key, 6), position), (blocks,), jnp.float32, least / len(split), top_value / len(split))
        gain = gain * jnp.repeat(jnp.exp(heights), extent[position] // blocks).reshape((-1,) + (1,) * (len(extent) - 1 - position))
    return gain


def scatter_about(key, shape, width, limit, cuts=(), kind=jnp.bfloat16):
    result = width * jax.random.normal(key, shape, jnp.float32)
    if cuts:
        result = result * block_scale(key, shape, cuts, -0.22, 0.18)
    return jnp.clip(result, -limit, limit).astype(kind)


def setup_inputs(seed: int = 0) -> dict:
    seeds = jax.random.split(jax.random.key(seed), 5)
    return {
        "tokens": draw_tokens(jax.random.fold_in(seeds[4], 71), 0),
        "codebook": draw_codebook(jax.random.fold_in(seeds[4], 71), 0),
        "cotangent": scatter_about(seeds[2], (TOKENS, D), 1.0, 6.0, ((0, 4),)),
        "indices": set_ends(jax.random.randint(seeds[3], (TOKENS,), 0, CODES), jax.random.fold_in(seeds[3], 1), 0, CODES - 1).astype(jnp.int32),
    }


def reference(tokens, codebook, cotangent, indices):
    blocks = codebook.reshape(CODES // CODE_DEV, CODE_DEV, D)
    dims = (((1,), (1,)), ((), ()))

    def first(carry, blk):
        top, total, weighted = carry
        logits = lax.dot_general(tokens, blk, dims, preferred_element_type=jnp.float32)
        back = lax.dot_general(cotangent, blk, dims, preferred_element_type=jnp.float32)
        newtop = jnp.maximum(top, jnp.max(logits, axis=1))
        factor = jnp.exp(top - newtop)
        expo = jnp.exp(logits - newtop[:, None])
        return (newtop, total * factor + jnp.sum(expo, axis=1), weighted * factor + jnp.sum(expo * back, axis=1)), None

    start = (jnp.full((TOKENS,), -jnp.inf, jnp.float32), jnp.zeros((TOKENS,), jnp.float32), jnp.zeros((TOKENS,), jnp.float32))
    (top, total, weighted), _ = lax.scan(first, start, blocks)
    ratio = weighted / total
    group_z = tokens.astype(jnp.float32).reshape(N_TOK, TOK_DEV, D)
    group_g = cotangent.astype(jnp.float32).reshape(N_TOK, TOK_DEV, D)

    def second(accum, item):
        blk, offset = item
        logits = lax.dot_general(tokens, blk, dims, preferred_element_type=jnp.float32)
        back = lax.dot_general(cotangent, blk, dims, preferred_element_type=jnp.float32)
        probs = jnp.exp(logits - top[:, None]) / total[:, None]
        dlogits = (probs * (back - ratio[:, None])).astype(jnp.bfloat16)
        accum = accum + jnp.dot(dlogits, blk, preferred_element_type=jnp.float32)
        onehot = (indices[:, None] == (offset + jnp.arange(CODE_DEV, dtype=jnp.int32))[None, :]).astype(jnp.float32)
        soft = dlogits.astype(jnp.float32).reshape(N_TOK, TOK_DEV, CODE_DEV)
        part = jnp.einsum('gtc,gtd->gcd', soft, group_z) + jnp.einsum('gtc,gtd->gcd', onehot.reshape(N_TOK, TOK_DEV, CODE_DEV), group_g)
        part = lax.optimization_barrier(part.astype(jnp.bfloat16)).astype(jnp.float32)
        return accum, jnp.sum(part, axis=0)

    offsets = jnp.arange(CODES // CODE_DEV, dtype=jnp.int32) * CODE_DEV
    grad_tokens, grads = lax.scan(second, jnp.zeros((TOKENS, D), jnp.float32), (blocks, offsets))
    return grad_tokens, grads.reshape(CODES, D)
```

```python
import functools

import jax
import jax.numpy as jnp
from jax import lax
from jax.experimental import pallas as pl
from jax.experimental.pallas import tpu as pltpu
from jax.sharding import PartitionSpec as P

MESH = pl.DeviceIdType.MESH
F32 = jnp.float32
BF16 = jnp.bfloat16
NT = (((1,), (1,)), ((), ()))

RING = 8
TOK = 1024
HALF = TOK // 2
CODES = 2048
D = 256
TILE = 256
TILES = CODES // TILE
QUARTER = CODES // 4
ROWS = D // 2 // RING


def to_grid(row):
    return jnp.concatenate([row[:, 128 * i : 128 * (i + 1)] for i in range(HALF // 128)], axis=0)


def to_row(grid):
    return jnp.concatenate([grid[i : i + 1] for i in range(HALF // 128)], axis=1)


def combine(parts):
    top = functools.reduce(jnp.maximum, [p[0:4] for p in parts])
    total = jnp.zeros_like(top)
    weighted = jnp.zeros_like(top)
    for p in parts:
        factor = jnp.exp(p[0:4] - top)
        total = total + p[4:8] * factor
        weighted = weighted + p[8:12] * factor
    return top, total, weighted


def kernel(
    tok_ref,
    cot_ref,
    cb_ref,
    idx_ref,
    grad_tok_ref,
    grad_cb_ref,
    expo,
    back,
    direct,
    cbt,
    uv_own,
    uv_other,
    uv_acc,
    uv_send,
    uv_recv,
    stat_own,
    stat_other,
    stat_1,
    stat_2,
    sum_2,
    final,
    cb_send,
    cb_recv,
    core_send,
    core_recv,
    ring_send,
    ring_recv,
    x_send,
    x_recv,
):
    code = lax.axis_index("code")
    x = lax.axis_index("tok")
    y, z, core = code // 16, (code // 2) % 8, code % 2
    other = (code + 1 - 2 * core, x)
    x_size = 4

    def along(axis, k):
        if axis == "z":
            return (y * 16 + ((z + k) % RING) * 2 + core, x)
        return (((y + k) % RING) * 16 + z * 2 + core, x)

    first = (("z", z), ("y", y))
    second = (("y", y), ("z", z))

    barrier = pltpu.get_barrier_semaphore()

    def greet(k, carry):
        for axis in ("z", "y"):
            pl.semaphore_signal(barrier, inc=1, device_id=along(axis, k), device_id_type=MESH)
        return carry

    lax.fori_loop(1, RING, greet, 0)
    for k in range(1, x_size):
        pl.semaphore_signal(barrier, inc=1, device_id=(code, (x + k) % x_size), device_id_type=MESH)
    pl.semaphore_signal(barrier, inc=1, device_id=other, device_id_type=MESH)

    def ring_copy(buf, stage, half, axis, me, k, src=None):
        slot = (me + k) % RING
        return pltpu.make_async_remote_copy(
            src_ref=buf.at[half, me] if src is None else src.at[half, slot],
            dst_ref=buf.at[half, me],
            send_sem=ring_send.at[stage, half, slot],
            recv_sem=ring_recv.at[stage, half, me],
            device_id=along(axis, k),
            device_id_type=MESH,
        )

    def ring_arrival(buf, stage, half, axis, me, k):
        slot = (me + k) % RING
        return pltpu.make_async_remote_copy(
            src_ref=buf.at[half, slot],
            dst_ref=buf.at[half, slot],
            send_sem=ring_send.at[stage, half, slot],
            recv_sem=ring_recv.at[stage, half, slot],
            device_id=along(axis, k),
            device_id_type=MESH,
        )

    def ring_start(buf, stage, order, src=None):
        def step(k, carry):
            for half in range(2):
                ring_copy(buf, stage, half, *order[half], k, src).start()
            return carry

        lax.fori_loop(1, RING, step, 0)

    def ring_wait(buf, stage, order):
        def step(k, carry):
            for half in range(2):
                ring_arrival(buf, stage, half, *order[half], k).wait_recv()
            return carry

        lax.fori_loop(1, RING, step, 0)

    def ring_drain(buf, stage, order, src=None):
        def step(k, carry):
            for half in range(2):
                ring_copy(buf, stage, half, *order[half], k, src).wait_send()
            return carry

        lax.fori_loop(1, RING, step, 0)

    def core_copy(src, dst, index):
        return pltpu.make_async_remote_copy(
            src_ref=src,
            dst_ref=dst,
            send_sem=core_send.at[index],
            recv_sem=core_recv.at[index],
            device_id=other,
            device_id_type=MESH,
        )

    def fold(value, op):
        return op(value.reshape(TILE // 8, 8, TOK), axis=0)

    def pass_logits(i, top):
        rows = pl.ds(pl.multiple_of(i * TILE, TILE), TILE)
        logits = lax.dot_general(cb_ref[rows], tok_ref[...], NT, preferred_element_type=F32)
        expo[rows] = logits
        return jnp.maximum(top, fold(logits, jnp.max))

    top = lax.fori_loop(0, TILES, pass_logits, jnp.full((8, TOK), -jnp.inf, F32))
    top = jnp.max(top, axis=0, keepdims=True)

    def pass_back(i, carry):
        total, weighted = carry
        rows = pl.ds(pl.multiple_of(i * TILE, TILE), TILE)
        proj = lax.dot_general(cb_ref[rows], cot_ref[...], NT, preferred_element_type=F32)
        back[rows] = proj
        e = jnp.exp(expo[rows] - top)
        expo[rows] = e
        return total + fold(e, jnp.sum), weighted + fold(e * proj, jnp.sum)

    zero = jnp.zeros((8, TOK), F32)
    total, weighted = lax.fori_loop(0, TILES, pass_back, (zero, zero))
    total = jnp.sum(total, axis=0, keepdims=True)
    weighted = jnp.sum(weighted, axis=0, keepdims=True)

    for half in range(2):
        span = slice(half * HALF, (half + 1) * HALF)
        stat_own[half, 0:4] = to_grid(top[:, span])
        stat_own[half, 4:8] = to_grid(total[:, span])
        stat_own[half, 8:12] = to_grid(weighted[:, span])
    pl.semaphore_wait(barrier, 2 * (RING - 1) + x_size - 1 + 1)
    stat_copy = core_copy(stat_own, stat_other, 0)
    stat_copy.start()

    def pass_turn(i, carry):
        rows = pl.ds(pl.multiple_of(i * TILE, TILE), TILE)
        cbt[:, rows] = cb_ref[rows].astype(F32).T.astype(BF16)
        return carry

    lax.fori_loop(0, TILES, pass_turn, 0)
    stat_copy.wait()

    scale, mean = [], []
    for half in range(2):
        states = [jnp.where(core == 0, a, b) for a, b in ((stat_own[half], stat_other[half]), (stat_other[half], stat_own[half]))]
        pair_top, pair_total, pair_weighted = combine(states)
        me = first[half][1]
        stat_1[half, me, 0:4] = pair_top
        stat_1[half, me, 4:8] = pair_total
        stat_1[half, me, 8:12] = pair_weighted
        scale.append(to_row(jnp.exp(stat_own[half, 0:4] - pair_top)))
        mean.append(to_row(pair_weighted / pair_total))
    ring_start(stat_1, 0, first)

    scale = jnp.concatenate(scale, axis=1)
    mean = jnp.concatenate(mean, axis=1)
    uv_acc[...] = jnp.zeros_like(uv_acc)

    def pass_uv(i, carry):
        rows = pl.ds(pl.multiple_of(i * TILE, TILE), TILE)
        e = expo[rows] * scale
        codes = cbt[:, rows]
        u = (e * (back[rows] - mean)).astype(BF16)
        uv_acc[0] += jnp.dot(codes, u, preferred_element_type=F32)
        uv_acc[1] += jnp.dot(codes, e.astype(BF16), preferred_element_type=F32)
        return carry

    lax.fori_loop(0, TILES, pass_uv, 0)
    for c in range(2):
        for which in range(2):
            for half in range(2):
                uv_own[c, which, half] = uv_acc[which, c * 128 : (c + 1) * 128, half * HALF : (half + 1) * HALF].astype(BF16)
    uv_copy = core_copy(uv_own.at[1 - core], uv_other, 1)
    uv_copy.start()
    uv_copy.wait()
    for half in range(2):
        me = first[half][1]
        for which in range(2):
            both = uv_own[core, which, half].astype(F32) + uv_other[which, half].astype(F32)
            for k in range(RING):
                uv_send[half, k, which] = both[k * ROWS : (k + 1) * ROWS].astype(BF16)
        uv_recv[half, me] = uv_send[half, me]
    ring_start(uv_recv, 1, first, uv_send)

    ring_wait(stat_1, 0, first)
    for half in range(2):
        ring_top, ring_total, ring_weighted = combine([stat_1[half, j] for j in range(RING)])
        me = second[half][1]
        stat_2[half, me, 0:4] = ring_top
        stat_2[half, me, 4:8] = ring_total
        stat_2[half, me, 8:12] = ring_weighted
    ring_start(stat_2, 2, second)

    def pass_direct(i, carry):
        rows = pl.ds(pl.multiple_of(i * TILE, TILE), TILE)
        slot = idx_ref[...] - (code * CODES + i * TILE)
        hot = lax.broadcasted_iota(jnp.int32, (TILE, TOK), 0) == slot
        hot = jnp.where(hot, 1.0, 0.0).astype(BF16)
        direct[rows] = jnp.dot(hot, cot_ref[...], preferred_element_type=F32)
        return carry

    lax.fori_loop(0, TILES, pass_direct, 0)

    ring_wait(stat_2, 2, second)
    state = [combine([stat_2[half, j] for j in range(RING)]) for half in range(2)]
    ratio = [w / t for _, t, w in state]
    local_scale = jnp.concatenate(
        [to_row(jnp.exp(stat_own[half, 0:4] - state[half][0]) / state[half][1]) for half in range(2)], axis=1
    )
    ratio_row = jnp.concatenate([to_row(ratio[half]) for half in range(2)], axis=1)

    def x_copy(k):
        return pltpu.make_async_remote_copy(
            src_ref=cb_send.at[k],
            dst_ref=cb_recv.at[k],
            send_sem=x_send.at[k],
            recv_sem=x_recv.at[k],
            device_id=(code, (x + k) % x_size),
            device_id_type=MESH,
        )

    def code_rows(k):
        base = ((x + k) % x_size) * QUARTER

        def step(i, carry):
            rows = pl.ds(pl.multiple_of(base + i * TILE, TILE), TILE)
            grad = (expo[rows] * local_scale * (back[rows] - ratio_row)).astype(BF16)
            part = jnp.dot(grad, tok_ref[...], preferred_element_type=F32) + direct[rows]
            cb_send[k, pl.ds(pl.multiple_of(i * TILE, TILE), TILE)] = part.astype(BF16)
            return carry

        lax.fori_loop(0, QUARTER // TILE, step, 0)

    code_rows(2)
    x_copy(2).start()

    ring_wait(uv_recv, 1, first)
    for half in range(2):
        acc = jnp.zeros((ROWS, HALF), F32)
        for j in range(RING):
            peer = stat_1[half, j]
            factor = jnp.exp(peer[0:4] - state[half][0]) / state[half][1]
            shift = peer[8:12] / peer[4:8] - ratio[half]
            acc = acc + to_row(factor) * (
                uv_recv[half, j, 0].astype(F32) + to_row(shift) * uv_recv[half, j, 1].astype(F32)
            )
        sum_2[half, second[half][1]] = acc.astype(BF16)
    ring_start(sum_2, 3, second)

    code_rows(1)
    x_copy(1).start()
    code_rows(3)
    x_copy(3).start()
    code_rows(0)

    ring_wait(sum_2, 3, second)
    for half in range(2):
        acc = functools.reduce(jnp.add, [sum_2[half, j].astype(F32) for j in range(RING)])
        final[core, half, first[half][1]] = acc.astype(BF16)

    def final_copy(half, k):
        axis, me = first[half]
        slot = (me + k) % RING
        return pltpu.make_async_remote_copy(
            src_ref=final.at[core, half, me],
            dst_ref=final.at[core, half, me],
            send_sem=ring_send.at[4, half, slot],
            recv_sem=ring_recv.at[4, half, me],
            device_id=along(axis, k),
            device_id_type=MESH,
        )

    def final_arrival(half, k):
        axis, me = first[half]
        slot = (me + k) % RING
        return pltpu.make_async_remote_copy(
            src_ref=final.at[core, half, slot],
            dst_ref=final.at[core, half, slot],
            send_sem=ring_send.at[4, half, slot],
            recv_sem=ring_recv.at[4, half, slot],
            device_id=along(axis, k),
            device_id_type=MESH,
        )

    def final_forward(half, slot, whose):
        return core_copy(final.at[whose, half, slot], final.at[whose, half, slot], 2 + half * RING + slot)

    def final_start(k, carry):
        for half in range(2):
            final_copy(half, k).start()
        return carry

    lax.fori_loop(1, RING, final_start, 0)
    for half in range(2):
        final_forward(half, first[half][1], core).start()

    def final_pass(k, carry):
        for half in range(2):
            final_arrival(half, k).wait_recv()
            final_forward(half, (first[half][1] + k) % RING, core).start()
        return carry

    lax.fori_loop(1, RING, final_pass, 0)

    for k in range(1, x_size):
        x_copy(k).wait_recv()
    acc = cb_send[0].astype(F32)
    for k in range(1, x_size):
        acc = acc + cb_recv[k].astype(F32)
    grad_cb_ref[...] = acc

    def final_end(k, carry):
        for half in range(2):
            final_forward(half, k, 1 - core).wait_recv()
            final_forward(half, k, core).wait_send()
        return carry

    lax.fori_loop(0, RING, final_end, 0)
    for half in range(2):
        for c in range(2):
            block = jnp.concatenate([final[c, half, j].astype(F32) for j in range(RING)], axis=0)
            grad_tok_ref[half * HALF : (half + 1) * HALF, c * 128 : (c + 1) * 128] = block.T

    ring_drain(stat_1, 0, first)
    ring_drain(uv_recv, 1, first, uv_send)
    ring_drain(stat_2, 2, second)
    ring_drain(sum_2, 3, second)

    def final_drain(k, carry):
        for half in range(2):
            final_copy(half, k).wait_send()
        return carry

    lax.fori_loop(1, RING, final_drain, 0)
    for k in range(1, x_size):
        x_copy(k).wait_send()


def shards(tokens, codebook, cotangent, indices):
    vmem = pl.BlockSpec(memory_space=pltpu.VMEM)
    return pl.pallas_call(
        kernel,
        out_shape=(
            jax.ShapeDtypeStruct((TOK, D), F32),
            jax.ShapeDtypeStruct((QUARTER, D), F32),
        ),
        in_specs=[vmem] * 4,
        out_specs=(vmem, vmem),
        scratch_shapes=[
            pltpu.VMEM((CODES, TOK), F32),
            pltpu.VMEM((CODES, TOK), F32),
            pltpu.VMEM((CODES, D), F32),
            pltpu.VMEM((D, CODES), BF16),
            pltpu.VMEM((2, 2, 2, 128, HALF), BF16),
            pltpu.VMEM((2, 2, 128, HALF), BF16),
            pltpu.VMEM((2, D, TOK), F32),
            pltpu.VMEM((2, RING, 2, ROWS, HALF), BF16),
            pltpu.VMEM((2, RING, 2, ROWS, HALF), BF16),
            pltpu.VMEM((2, 12, 128), F32),
            pltpu.VMEM((2, 12, 128), F32),
            pltpu.VMEM((2, RING, 12, 128), F32),
            pltpu.VMEM((2, RING, 12, 128), F32),
            pltpu.VMEM((2, RING, ROWS, HALF), BF16),
            pltpu.VMEM((2, 2, RING, ROWS, HALF), BF16),
            pltpu.VMEM((4, QUARTER, D), BF16),
            pltpu.VMEM((4, QUARTER, D), BF16),
            pltpu.SemaphoreType.DMA((2 + 2 * RING,)),
            pltpu.SemaphoreType.DMA((2 + 2 * RING,)),
            pltpu.SemaphoreType.DMA((5, 2, RING)),
            pltpu.SemaphoreType.DMA((5, 2, RING)),
            pltpu.SemaphoreType.DMA((4,)),
            pltpu.SemaphoreType.DMA((4,)),
        ],
        compiler_params=pltpu.CompilerParams(
            collective_id=0, has_side_effects=True, vmem_limit_bytes=56 * 1024 * 1024
        ),
        name="quantizer_backward",
    )(tokens, cotangent, codebook, indices.reshape(1, TOK))


def solution(mesh):
    return jax.shard_map(
        shards,
        mesh=mesh,
        in_specs=(P("tok", None), P("code", None), P("tok", None), P("tok")),
        out_specs=(P("tok", None), P(("code", "tok"), None)),
        check_vma=False,
    )
```

```python
import functools

import jax
import jax.numpy as jnp
from jax import lax
from jax.experimental import pallas as pl
from jax.experimental.pallas import tpu as pltpu
from jax.sharding import PartitionSpec as P

MESH = pl.DeviceIdType.MESH
F32 = jnp.float32
BF16 = jnp.bfloat16
NT = (((1,), (1,)), ((), ()))

RING = 8
TOK = 1024
HALF = TOK // 2
CODES = 2048
D = 256
VMEM_LIMIT = 44 * 1024 * 1024
QUARTER = CODES // 4
ROWS = D // 2 // RING


def to_grid(row):
    return jnp.concatenate([row[:, 128 * i : 128 * (i + 1)] for i in range(HALF // 128)], axis=0)


def to_row(grid):
    return jnp.concatenate([grid[i : i + 1] for i in range(HALF // 128)], axis=1)


def combine(parts):
    top = functools.reduce(jnp.maximum, [p[0:4] for p in parts])
    total = jnp.zeros_like(top)
    weighted = jnp.zeros_like(top)
    for p in parts:
        factor = jnp.exp(p[0:4] - top)
        total = total + p[4:8] * factor
        weighted = weighted + p[8:12] * factor
    return top, total, weighted


def kernel(
    tok_hbm,
    cot_hbm,
    cb_hbm,
    idx_hbm,
    grad_tok_ref,
    grad_cb_ref,
    tok_ref,
    cot_ref,
    cb_ref,
    idx_ref,
    load_sem,
    expo,
    back,
    direct,
    cbt,
    uv_own,
    uv_other,
    uv_send,
    uv_recv,
    stat_own,
    stat_other,
    stat_1,
    stat_2,
    sum_2,
    final,
    cb_send,
    cb_recv,
    core_send,
    core_recv,
    ring_send,
    ring_recv,
    x_send,
    x_recv,
):
    code = lax.axis_index("code")
    x = lax.axis_index("tok")
    y, z, core = code // 16, (code // 2) % 8, code % 2
    other = (code + 1 - 2 * core, x)
    x_size = 4

    def along(axis, k):
        if axis == "z":
            return (y * 16 + ((z + k) % RING) * 2 + core, x)
        return (((y + k) % RING) * 16 + z * 2 + core, x)

    loads = [
        pltpu.make_async_copy(src, dst, load_sem.at[i])
        for i, (src, dst) in enumerate(
            ((cb_hbm, cb_ref), (tok_hbm, tok_ref), (cot_hbm, cot_ref), (idx_hbm, idx_ref))
        )
    ]
    for load in loads:
        load.start()

    first = (("z", z), ("y", y))
    second = (("y", y), ("z", z))

    barrier = pltpu.get_barrier_semaphore()

    def greet(k, carry):
        for axis in ("z", "y"):
            pl.semaphore_signal(barrier, inc=1, device_id=along(axis, k), device_id_type=MESH)
        return carry

    lax.fori_loop(1, RING, greet, 0)
    for k in range(1, x_size):
        pl.semaphore_signal(barrier, inc=1, device_id=(code, (x + k) % x_size), device_id_type=MESH)
    pl.semaphore_signal(barrier, inc=1, device_id=other, device_id_type=MESH)

    def ring_copy(buf, stage, half, axis, me, k, src=None):
        slot = (me + k) % RING
        return pltpu.make_async_remote_copy(
            src_ref=buf.at[half, me] if src is None else src.at[half, slot],
            dst_ref=buf.at[half, me],
            send_sem=ring_send.at[stage, half, slot],
            recv_sem=ring_recv.at[stage, half, me],
            device_id=along(axis, k),
            device_id_type=MESH,
        )

    def ring_arrival(buf, stage, half, axis, me, k):
        slot = (me + k) % RING
        return pltpu.make_async_remote_copy(
            src_ref=buf.at[half, slot],
            dst_ref=buf.at[half, slot],
            send_sem=ring_send.at[stage, half, slot],
            recv_sem=ring_recv.at[stage, half, slot],
            device_id=along(axis, k),
            device_id_type=MESH,
        )

    def ring_start(buf, stage, order, src=None):
        def step(k, carry):
            for half in range(2):
                ring_copy(buf, stage, half, *order[half], k, src).start()
            return carry

        lax.fori_loop(1, RING, step, 0)

    def ring_wait(buf, stage, order):
        def step(k, carry):
            for half in range(2):
                ring_arrival(buf, stage, half, *order[half], k).wait_recv()
            return carry

        lax.fori_loop(1, RING, step, 0)

    def ring_drain(buf, stage, order, src=None):
        def step(k, carry):
            for half in range(2):
                ring_copy(buf, stage, half, *order[half], k, src).wait_send()
            return carry

        lax.fori_loop(1, RING, step, 0)

    def core_copy(src, dst, index):
        return pltpu.make_async_remote_copy(
            src_ref=src,
            dst_ref=dst,
            send_sem=core_send.at[index],
            recv_sem=core_recv.at[index],
            device_id=other,
            device_id_type=MESH,
        )

    def fold(value, op):
        return op(value.reshape(CODES // 8, 8, TOK), axis=0)

    loads[0].wait()
    loads[1].wait()
    logits = lax.dot_general(cb_ref[...], tok_ref[...], NT, preferred_element_type=F32)
    expo[...] = logits
    loads[2].wait()
    back[...] = lax.dot_general(cb_ref[...], cot_ref[...], NT, preferred_element_type=F32)
    top = jnp.max(fold(logits, jnp.max), axis=0, keepdims=True)
    e = jnp.exp(expo[...] - top)
    expo[...] = e
    total = jnp.sum(fold(e, jnp.sum), axis=0, keepdims=True)
    weighted = jnp.sum(fold(e * back[...], jnp.sum), axis=0, keepdims=True)

    for half in range(2):
        span = slice(half * HALF, (half + 1) * HALF)
        stat_own[half, 0:4] = to_grid(top[:, span])
        stat_own[half, 4:8] = to_grid(total[:, span])
        stat_own[half, 8:12] = to_grid(weighted[:, span])
    pl.semaphore_wait(barrier, 2 * (RING - 1) + x_size - 1 + 1)
    stat_copy = core_copy(stat_own, stat_other, 0)
    stat_copy.start()

    cbt[...] = cb_ref[...].T
    stat_copy.wait()

    scale, mean = [], []
    for half in range(2):
        states = [jnp.where(core == 0, a, b) for a, b in ((stat_own[half], stat_other[half]), (stat_other[half], stat_own[half]))]
        pair_top, pair_total, pair_weighted = combine(states)
        me = first[half][1]
        stat_1[half, me, 0:4] = pair_top
        stat_1[half, me, 4:8] = pair_total
        stat_1[half, me, 8:12] = pair_weighted
        scale.append(to_row(jnp.exp(stat_own[half, 0:4] - pair_top)))
        mean.append(to_row(pair_weighted / pair_total))
    ring_start(stat_1, 0, first)

    for half in range(2):
        span = slice(half * HALF, (half + 1) * HALF)
        e = expo[:, span] * scale[half]
        u = (e * (back[:, span] - mean[half])).astype(BF16)
        for which, weight in ((0, u), (1, e.astype(BF16))):
            value = jnp.dot(cbt[...], weight, preferred_element_type=F32).astype(BF16)
            for c in range(2):
                uv_own[c, which, half] = value[c * 128 : (c + 1) * 128]
    uv_copy = core_copy(uv_own.at[1 - core], uv_other, 1)
    uv_copy.start()
    uv_copy.wait()
    for half in range(2):
        me = first[half][1]
        for which in range(2):
            both = uv_own[core, which, half].astype(F32) + uv_other[which, half].astype(F32)
            for k in range(RING):
                uv_send[half, k, which] = both[k * ROWS : (k + 1) * ROWS].astype(BF16)
        uv_recv[half, me] = uv_send[half, me]
    ring_start(uv_recv, 1, first, uv_send)

    ring_wait(stat_1, 0, first)
    for half in range(2):
        ring_top, ring_total, ring_weighted = combine([stat_1[half, j] for j in range(RING)])
        me = second[half][1]
        stat_2[half, me, 0:4] = ring_top
        stat_2[half, me, 4:8] = ring_total
        stat_2[half, me, 8:12] = ring_weighted
    ring_start(stat_2, 2, second)

    loads[3].wait()
    hot = lax.broadcasted_iota(jnp.int32, (CODES, TOK), 0) == idx_ref[...] - code * CODES
    hot = jnp.where(hot, 1.0, 0.0).astype(BF16)
    direct[...] = jnp.dot(hot, cot_ref[...], preferred_element_type=F32)

    ring_wait(stat_2, 2, second)
    state = [combine([stat_2[half, j] for j in range(RING)]) for half in range(2)]
    ratio = [w / t for _, t, w in state]
    local_scale = jnp.concatenate(
        [to_row(jnp.exp(stat_own[half, 0:4] - state[half][0]) / state[half][1]) for half in range(2)], axis=1
    )
    ratio_row = jnp.concatenate([to_row(ratio[half]) for half in range(2)], axis=1)

    def x_copy(k):
        return pltpu.make_async_remote_copy(
            src_ref=cb_send.at[k],
            dst_ref=cb_recv.at[k],
            send_sem=x_send.at[k],
            recv_sem=x_recv.at[k],
            device_id=(code, (x + k) % x_size),
            device_id_type=MESH,
        )

    def code_rows(k):
        rows = pl.ds(pl.multiple_of(((x + k) % x_size) * QUARTER, QUARTER), QUARTER)
        grad = (expo[rows] * local_scale * (back[rows] - ratio_row)).astype(BF16)
        part = jnp.dot(grad, tok_ref[...], preferred_element_type=F32) + direct[rows]
        cb_send[k] = part.astype(BF16)

    code_rows(2)
    x_copy(2).start()

    ring_wait(uv_recv, 1, first)
    for half in range(2):
        acc = jnp.zeros((ROWS, HALF), F32)
        for j in range(RING):
            peer = stat_1[half, j]
            factor = jnp.exp(peer[0:4] - state[half][0]) / state[half][1]
            shift = peer[8:12] / peer[4:8] - ratio[half]
            acc = acc + to_row(factor) * (
                uv_recv[half, j, 0].astype(F32) + to_row(shift) * uv_recv[half, j, 1].astype(F32)
            )
        sum_2[half, second[half][1]] = acc.astype(BF16)
    ring_start(sum_2, 3, second)

    code_rows(1)
    x_copy(1).start()
    code_rows(3)
    x_copy(3).start()
    code_rows(0)

    ring_wait(sum_2, 3, second)
    for half in range(2):
        acc = functools.reduce(jnp.add, [sum_2[half, j].astype(F32) for j in range(RING)])
        final[core, half, first[half][1]] = acc.astype(BF16)

    def final_copy(half, k):
        axis, me = first[half]
        slot = (me + k) % RING
        return pltpu.make_async_remote_copy(
            src_ref=final.at[core, half, me],
            dst_ref=final.at[core, half, me],
            send_sem=ring_send.at[4, half, slot],
            recv_sem=ring_recv.at[4, half, me],
            device_id=along(axis, k),
            device_id_type=MESH,
        )

    def final_arrival(half, k):
        axis, me = first[half]
        slot = (me + k) % RING
        return pltpu.make_async_remote_copy(
            src_ref=final.at[core, half, slot],
            dst_ref=final.at[core, half, slot],
            send_sem=ring_send.at[4, half, slot],
            recv_sem=ring_recv.at[4, half, slot],
            device_id=along(axis, k),
            device_id_type=MESH,
        )

    def final_forward(half, slot, whose):
        return core_copy(final.at[whose, half, slot], final.at[whose, half, slot], 2 + half * RING + slot)

    def final_start(k, carry):
        for half in range(2):
            final_copy(half, k).start()
        return carry

    lax.fori_loop(1, RING, final_start, 0)
    for half in range(2):
        final_forward(half, first[half][1], core).start()

    def final_pass(k, carry):
        for half in range(2):
            final_arrival(half, k).wait_recv()
            final_forward(half, (first[half][1] + k) % RING, core).start()
        return carry

    lax.fori_loop(1, RING, final_pass, 0)

    for k in range(1, x_size):
        x_copy(k).wait_recv()
    acc = cb_send[0].astype(F32)
    for k in range(1, x_size):
        acc = acc + cb_recv[k].astype(F32)
    grad_cb_ref[...] = acc

    def final_end(k, carry):
        for half in range(2):
            final_forward(half, k, 1 - core).wait_recv()
            final_forward(half, k, core).wait_send()
        return carry

    lax.fori_loop(0, RING, final_end, 0)
    for half in range(2):
        for c in range(2):
            block = jnp.concatenate([final[c, half, j].astype(F32) for j in range(RING)], axis=0)
            grad_tok_ref[half * HALF : (half + 1) * HALF, c * 128 : (c + 1) * 128] = block.T

    ring_drain(stat_1, 0, first)
    ring_drain(uv_recv, 1, first, uv_send)
    ring_drain(stat_2, 2, second)
    ring_drain(sum_2, 3, second)

    def final_drain(k, carry):
        for half in range(2):
            final_copy(half, k).wait_send()
        return carry

    lax.fori_loop(1, RING, final_drain, 0)
    for k in range(1, x_size):
        x_copy(k).wait_send()


def write(grad_tok_ref, grad_cb_ref, tok_out, cb_out, sems):
    copies = [
        pltpu.make_async_copy(grad_tok_ref, tok_out, sems.at[0]),
        pltpu.make_async_copy(grad_cb_ref, cb_out, sems.at[1]),
    ]
    for copy in copies:
        copy.start()
    for copy in copies:
        copy.wait()


def shards(tokens, codebook, cotangent, indices):
    vmem = pl.BlockSpec(memory_space=pltpu.VMEM)
    hbm = pl.BlockSpec(memory_space=pltpu.HBM)
    shapes = (
        jax.ShapeDtypeStruct((TOK, D), F32),
        jax.ShapeDtypeStruct((QUARTER, D), F32),
    )
    grads = pl.pallas_call(
        kernel,
        out_shape=shapes,
        in_specs=[hbm] * 4,
        out_specs=(vmem, vmem),
        scratch_shapes=[
            pltpu.VMEM((TOK, D), BF16),
            pltpu.VMEM((TOK, D), BF16),
            pltpu.VMEM((CODES, D), BF16),
            pltpu.VMEM((1, TOK), jnp.int32),
            pltpu.SemaphoreType.DMA((4,)),
            pltpu.VMEM((CODES, TOK), F32),
            pltpu.VMEM((CODES, TOK), F32),
            pltpu.VMEM((CODES, D), F32),
            pltpu.VMEM((D, CODES), BF16),
            pltpu.VMEM((2, 2, 2, 128, HALF), BF16),
            pltpu.VMEM((2, 2, 128, HALF), BF16),
            pltpu.VMEM((2, RING, 2, ROWS, HALF), BF16),
            pltpu.VMEM((2, RING, 2, ROWS, HALF), BF16),
            pltpu.VMEM((2, 12, 128), F32),
            pltpu.VMEM((2, 12, 128), F32),
            pltpu.VMEM((2, RING, 12, 128), F32),
            pltpu.VMEM((2, RING, 12, 128), F32),
            pltpu.VMEM((2, RING, ROWS, HALF), BF16),
            pltpu.VMEM((2, 2, RING, ROWS, HALF), BF16),
            pltpu.VMEM((4, QUARTER, D), BF16),
            pltpu.VMEM((4, QUARTER, D), BF16),
            pltpu.SemaphoreType.DMA((2 + 2 * RING,)),
            pltpu.SemaphoreType.DMA((2 + 2 * RING,)),
            pltpu.SemaphoreType.DMA((5, 2, RING)),
            pltpu.SemaphoreType.DMA((5, 2, RING)),
            pltpu.SemaphoreType.DMA((4,)),
            pltpu.SemaphoreType.DMA((4,)),
        ],
        compiler_params=pltpu.CompilerParams(
            collective_id=0, has_side_effects=True, vmem_limit_bytes=VMEM_LIMIT
        ),
        name="quantizer_backward",
    )(*(pltpu.with_memory_space_constraint(a, pltpu.HBM) for a in (tokens, cotangent, codebook, indices.reshape(1, TOK))))
    return pl.pallas_call(
        write,
        out_shape=shapes,
        in_specs=[vmem, vmem],
        out_specs=(hbm, hbm),
        scratch_shapes=[pltpu.SemaphoreType.DMA((2,))],
        compiler_params=pltpu.CompilerParams(vmem_limit_bytes=8 * 1024 * 1024),
        name="write_out",
    )(*grads)


def solution(mesh):
    return jax.shard_map(
        shards,
        mesh=mesh,
        in_specs=(P("tok", None), P("code", None), P("tok", None), P("tok")),
        out_specs=(P("tok", None), P(("code", "tok"), None)),
        check_vma=False,
    )
```

```python
import functools

import jax
import jax.numpy as jnp
from jax import lax
from jax.experimental import pallas as pl
from jax.experimental.pallas import tpu as pltpu
from jax.sharding import PartitionSpec as P

MESH = pl.DeviceIdType.MESH
F32 = jnp.float32
BF16 = jnp.bfloat16
NT = (((1,), (1,)), ((), ()))

RING = 8
FAR_FIRST = (4, 3, 5, 2, 6, 1, 7)
TOK = 1024
HALF = TOK // 2
CODES = 2048
D = 256
VMEM_LIMIT = 44 * 1024 * 1024
QUARTER = CODES // 4
ROWS = D // 2 // RING


def to_grid(row):
    return jnp.concatenate([row[:, 128 * i : 128 * (i + 1)] for i in range(HALF // 128)], axis=0)


def to_row(grid):
    return jnp.concatenate([grid[i : i + 1] for i in range(HALF // 128)], axis=1)


def combine(parts):
    top = functools.reduce(jnp.maximum, [p[0:4] for p in parts])
    total = jnp.zeros_like(top)
    weighted = jnp.zeros_like(top)
    for p in parts:
        factor = jnp.exp(p[0:4] - top)
        total = total + p[4:8] * factor
        weighted = weighted + p[8:12] * factor
    return top, total, weighted


def kernel(
    tok_hbm,
    cot_hbm,
    cb_hbm,
    idx_hbm,
    grad_tok_ref,
    grad_cb_ref,
    tok_ref,
    cot_ref,
    cb_ref,
    idx_ref,
    load_sem,
    expo,
    back,
    direct,
    cbt,
    uv_own,
    uv_other,
    uv_send,
    uv_recv,
    stat_own,
    stat_other,
    stat_1,
    stat_2,
    sum_2,
    final,
    cb_send,
    cb_recv,
    far_recv,
    cb_own,
    core_send,
    core_recv,
    ring_send,
    ring_recv,
    x_send,
    x_recv,
):
    code = lax.axis_index("code")
    x = lax.axis_index("tok")
    y, z, core = code // 16, (code // 2) % 8, code % 2
    other = (code + 1 - 2 * core, x)
    x_size = 4

    def along(axis, k):
        if axis == "z":
            return (y * 16 + ((z + k) % RING) * 2 + core, x)
        return (((y + k) % RING) * 16 + z * 2 + core, x)

    loads = [
        pltpu.make_async_copy(src, dst, load_sem.at[i])
        for i, (src, dst) in enumerate(
            ((cb_hbm, cb_ref), (tok_hbm, tok_ref), (cot_hbm, cot_ref), (idx_hbm, idx_ref))
        )
    ]
    for load in loads:
        load.start()

    first = (("z", z), ("y", y))
    second = (("y", y), ("z", z))

    barrier = pltpu.get_barrier_semaphore()

    def greet(k, carry):
        for axis in ("z", "y"):
            pl.semaphore_signal(barrier, inc=1, device_id=along(axis, k), device_id_type=MESH)
        return carry

    lax.fori_loop(1, RING, greet, 0)
    for k in (1, x_size - 1):
        pl.semaphore_signal(barrier, inc=1, device_id=(code, (x + k) % x_size), device_id_type=MESH)
    pl.semaphore_signal(barrier, inc=1, device_id=other, device_id_type=MESH)

    def ring_copy(buf, stage, half, axis, me, k, src=None):
        slot = (me + k) % RING
        return pltpu.make_async_remote_copy(
            src_ref=buf.at[half, me] if src is None else src.at[half, slot],
            dst_ref=buf.at[half, me],
            send_sem=ring_send.at[stage, half, slot],
            recv_sem=ring_recv.at[stage, half, me],
            device_id=along(axis, k),
            device_id_type=MESH,
        )

    def ring_arrival(buf, stage, half, axis, me, k):
        slot = (me + k) % RING
        return pltpu.make_async_remote_copy(
            src_ref=buf.at[half, slot],
            dst_ref=buf.at[half, slot],
            send_sem=ring_send.at[stage, half, slot],
            recv_sem=ring_recv.at[stage, half, slot],
            device_id=along(axis, k),
            device_id_type=MESH,
        )

    def ring_start(buf, stage, order, src=None, halves=(0, 1)):
        for k in FAR_FIRST:
            for half in halves:
                ring_copy(buf, stage, half, *order[half], k, src).start()

    def ring_wait(buf, stage, order):
        for k in reversed(FAR_FIRST):
            for half in range(2):
                ring_arrival(buf, stage, half, *order[half], k).wait_recv()

    def ring_drain(buf, stage, order, src=None):
        def step(k, carry):
            for half in range(2):
                ring_copy(buf, stage, half, *order[half], k, src).wait_send()
            return carry

        lax.fori_loop(1, RING, step, 0)

    def core_copy(src, dst, index):
        return pltpu.make_async_remote_copy(
            src_ref=src,
            dst_ref=dst,
            send_sem=core_send.at[index],
            recv_sem=core_recv.at[index],
            device_id=other,
            device_id_type=MESH,
        )

    def fold(value, op):
        return op(value.reshape(CODES // 8, 8, TOK), axis=0)

    loads[0].wait()
    loads[1].wait()
    logits = lax.dot_general(cb_ref[...], tok_ref[...], NT, preferred_element_type=F32)
    expo[...] = logits
    loads[2].wait()
    back[...] = lax.dot_general(cb_ref[...], cot_ref[...], NT, preferred_element_type=F32)
    top = jnp.max(fold(logits, jnp.max), axis=0, keepdims=True)
    e = jnp.exp(expo[...] - top)
    expo[...] = e
    total = jnp.sum(fold(e, jnp.sum), axis=0, keepdims=True)
    weighted = jnp.sum(fold(e * back[...], jnp.sum), axis=0, keepdims=True)

    for half in range(2):
        span = slice(half * HALF, (half + 1) * HALF)
        stat_own[half, 0:4] = to_grid(top[:, span])
        stat_own[half, 4:8] = to_grid(total[:, span])
        stat_own[half, 8:12] = to_grid(weighted[:, span])
    pl.semaphore_wait(barrier, 2 * (RING - 1) + 2 + 1)
    stat_copy = core_copy(stat_own, stat_other, 0)
    stat_copy.start()

    cbt[...] = cb_ref[...].T
    stat_copy.wait()

    scale, mean = [], []
    for half in range(2):
        states = [jnp.where(core == 0, a, b) for a, b in ((stat_own[half], stat_other[half]), (stat_other[half], stat_own[half]))]
        pair_top, pair_total, pair_weighted = combine(states)
        me = first[half][1]
        stat_1[half, me, 0:4] = pair_top
        stat_1[half, me, 4:8] = pair_total
        stat_1[half, me, 8:12] = pair_weighted
        scale.append(to_row(jnp.exp(stat_own[half, 0:4] - pair_top)))
        mean.append(to_row(pair_weighted / pair_total))
    ring_start(stat_1, 0, first)

    uv_copies = [core_copy(uv_own.at[half, 1 - core], uv_other.at[half], 1 + half) for half in range(2)]

    for half in range(2):
        span = slice(half * HALF, (half + 1) * HALF)
        e = expo[:, span] * scale[half]
        u = (e * (back[:, span] - mean[half])).astype(BF16)
        for which, weight in ((0, u), (1, e.astype(BF16))):
            value = jnp.dot(cbt[...], weight, preferred_element_type=F32).astype(BF16)
            for c in range(2):
                uv_own[half, c, which] = value[c * 128 : (c + 1) * 128]
        uv_copies[half].start()

    def uv_ring(half):
        uv_copies[half].wait()
        me = first[half][1]
        for which in range(2):
            both = uv_own[half, core, which].astype(F32) + uv_other[half, which].astype(F32)
            for k in range(RING):
                uv_send[half, k, which] = both[k * ROWS : (k + 1) * ROWS].astype(BF16)
        uv_recv[half, me] = uv_send[half, me]
        ring_start(uv_recv, 1, first, uv_send, (half,))

    uv_ring(0)

    ring_wait(stat_1, 0, first)
    for half in range(2):
        ring_top, ring_total, ring_weighted = combine([stat_1[half, j] for j in range(RING)])
        me = second[half][1]
        stat_2[half, me, 0:4] = ring_top
        stat_2[half, me, 4:8] = ring_total
        stat_2[half, me, 8:12] = ring_weighted
    ring_start(stat_2, 2, second)
    uv_ring(1)

    loads[3].wait()
    hot = lax.broadcasted_iota(jnp.int32, (CODES, TOK), 0) == idx_ref[...] - code * CODES
    hot = jnp.where(hot, 1.0, 0.0).astype(BF16)
    direct[...] = jnp.dot(hot, cot_ref[...], preferred_element_type=F32)

    ring_wait(stat_2, 2, second)
    state = [combine([stat_2[half, j] for j in range(RING)]) for half in range(2)]
    ratio = [w / t for _, t, w in state]
    local_scale = jnp.concatenate(
        [to_row(jnp.exp(stat_own[half, 0:4] - state[half][0]) / state[half][1]) for half in range(2)], axis=1
    )
    ratio_row = jnp.concatenate([to_row(ratio[half]) for half in range(2)], axis=1)

    low, high = pl.ds(0, QUARTER // 2), pl.ds(QUARTER // 2, QUARTER // 2)

    def x_copy(src, dst, index, side):
        return pltpu.make_async_remote_copy(
            src_ref=src,
            dst_ref=dst,
            send_sem=x_send.at[index],
            recv_sem=x_recv.at[index],
            device_id=(code, (x + (1, x_size - 1)[side]) % x_size),
            device_id_type=MESH,
        )

    far_copies = [x_copy(cb_send.at[2, part], far_recv.at[side], side, side) for side, part in ((0, low), (1, high))]
    near_copies = [
        x_copy(cb_send.at[side, part], cb_recv.at[side, part], 2 + side, side) for side, part in ((0, high), (1, low))
    ]
    sum_copies = [
        x_copy(cb_send.at[side, part], cb_recv.at[side, part], 4 + side, side) for side, part in ((0, low), (1, high))
    ]

    def code_rows(k):
        rows = pl.ds(pl.multiple_of(((x + k) % x_size) * QUARTER, QUARTER), QUARTER)
        grad = (expo[rows] * local_scale * (back[rows] - ratio_row)).astype(BF16)
        return jnp.dot(grad, tok_ref[...], preferred_element_type=F32) + direct[rows]

    cb_send[2] = code_rows(2).astype(BF16)
    for copy in far_copies:
        copy.start()

    ring_wait(uv_recv, 1, first)
    for half in range(2):
        acc = jnp.zeros((ROWS, HALF), F32)
        for j in range(RING):
            peer = stat_1[half, j]
            factor = jnp.exp(peer[0:4] - state[half][0]) / state[half][1]
            shift = peer[8:12] / peer[4:8] - ratio[half]
            acc = acc + to_row(factor) * (
                uv_recv[half, j, 0].astype(F32) + to_row(shift) * uv_recv[half, j, 1].astype(F32)
            )
        sum_2[half, second[half][1]] = acc.astype(BF16)
    ring_start(sum_2, 3, second)

    mid = QUARTER // 2
    part = code_rows(1)
    cb_send[0, high] = part[mid:].astype(BF16)
    near_copies[0].start()
    cb_own[0] = part[:mid]
    part = code_rows(3)
    cb_send[1, low] = part[:mid].astype(BF16)
    near_copies[1].start()
    cb_own[1] = part[mid:]
    for side, part in ((0, low), (1, high)):
        far_copies[side].wait_recv()
        cb_send[side, part] = (cb_own[side] + far_recv[side].astype(F32)).astype(BF16)
        sum_copies[side].start()
    grad_cb_ref[...] = code_rows(0)

    ring_wait(sum_2, 3, second)
    for half in range(2):
        acc = functools.reduce(jnp.add, [sum_2[half, j].astype(F32) for j in range(RING)])
        final[core, half, first[half][1]] = acc.astype(BF16)

    def final_copy(half, k):
        axis, me = first[half]
        slot = (me + k) % RING
        return pltpu.make_async_remote_copy(
            src_ref=final.at[core, half, me],
            dst_ref=final.at[core, half, me],
            send_sem=ring_send.at[4, half, slot],
            recv_sem=ring_recv.at[4, half, me],
            device_id=along(axis, k),
            device_id_type=MESH,
        )

    def final_arrival(half, k):
        axis, me = first[half]
        slot = (me + k) % RING
        return pltpu.make_async_remote_copy(
            src_ref=final.at[core, half, slot],
            dst_ref=final.at[core, half, slot],
            send_sem=ring_send.at[4, half, slot],
            recv_sem=ring_recv.at[4, half, slot],
            device_id=along(axis, k),
            device_id_type=MESH,
        )

    def final_forward(half, slot, whose):
        return core_copy(final.at[whose, half, slot], final.at[whose, half, slot], 3 + half * RING + slot)

    for k in FAR_FIRST:
        for half in range(2):
            final_copy(half, k).start()
    for half in range(2):
        final_forward(half, first[half][1], core).start()
    for k in reversed(FAR_FIRST):
        for half in range(2):
            final_arrival(half, k).wait_recv()
            final_forward(half, (first[half][1] + k) % RING, core).start()

    for copy in near_copies + sum_copies:
        copy.wait_recv()
    grad_cb_ref[...] += cb_recv[0].astype(F32) + cb_recv[1].astype(F32)

    def final_end(k, carry):
        for half in range(2):
            final_forward(half, k, 1 - core).wait_recv()
            final_forward(half, k, core).wait_send()
        return carry

    lax.fori_loop(0, RING, final_end, 0)
    for half in range(2):
        for c in range(2):
            block = jnp.concatenate([final[c, half, j].astype(F32) for j in range(RING)], axis=0)
            grad_tok_ref[half * HALF : (half + 1) * HALF, c * 128 : (c + 1) * 128] = block.T

    ring_drain(stat_1, 0, first)
    ring_drain(uv_recv, 1, first, uv_send)
    ring_drain(stat_2, 2, second)
    ring_drain(sum_2, 3, second)

    def final_drain(k, carry):
        for half in range(2):
            final_copy(half, k).wait_send()
        return carry

    lax.fori_loop(1, RING, final_drain, 0)
    for copy in far_copies + near_copies + sum_copies:
        copy.wait_send()


def write(grad_tok_ref, grad_cb_ref, tok_out, cb_out, sems):
    copies = [
        pltpu.make_async_copy(grad_tok_ref, tok_out, sems.at[0]),
        pltpu.make_async_copy(grad_cb_ref, cb_out, sems.at[1]),
    ]
    for copy in copies:
        copy.start()
    for copy in copies:
        copy.wait()


def shards(tokens, codebook, cotangent, indices):
    vmem = pl.BlockSpec(memory_space=pltpu.VMEM)
    hbm = pl.BlockSpec(memory_space=pltpu.HBM)
    shapes = (
        jax.ShapeDtypeStruct((TOK, D), F32),
        jax.ShapeDtypeStruct((QUARTER, D), F32),
    )
    grads = pl.pallas_call(
        kernel,
        out_shape=shapes,
        in_specs=[hbm] * 4,
        out_specs=(vmem, vmem),
        scratch_shapes=[
            pltpu.VMEM((TOK, D), BF16),
            pltpu.VMEM((TOK, D), BF16),
            pltpu.VMEM((CODES, D), BF16),
            pltpu.VMEM((1, TOK), jnp.int32),
            pltpu.SemaphoreType.DMA((4,)),
            pltpu.VMEM((CODES, TOK), F32),
            pltpu.VMEM((CODES, TOK), F32),
            pltpu.VMEM((CODES, D), F32),
            pltpu.VMEM((D, CODES), BF16),
            pltpu.VMEM((2, 2, 2, 128, HALF), BF16),
            pltpu.VMEM((2, 2, 128, HALF), BF16),
            pltpu.VMEM((2, RING, 2, ROWS, HALF), BF16),
            pltpu.VMEM((2, RING, 2, ROWS, HALF), BF16),
            pltpu.VMEM((2, 12, 128), F32),
            pltpu.VMEM((2, 12, 128), F32),
            pltpu.VMEM((2, RING, 12, 128), F32),
            pltpu.VMEM((2, RING, 12, 128), F32),
            pltpu.VMEM((2, RING, ROWS, HALF), BF16),
            pltpu.VMEM((2, 2, RING, ROWS, HALF), BF16),
            pltpu.VMEM((3, QUARTER, D), BF16),
            pltpu.VMEM((2, QUARTER, D), BF16),
            pltpu.VMEM((2, QUARTER // 2, D), BF16),
            pltpu.VMEM((2, QUARTER // 2, D), F32),
            pltpu.SemaphoreType.DMA((3 + 2 * RING,)),
            pltpu.SemaphoreType.DMA((3 + 2 * RING,)),
            pltpu.SemaphoreType.DMA((5, 2, RING)),
            pltpu.SemaphoreType.DMA((5, 2, RING)),
            pltpu.SemaphoreType.DMA((6,)),
            pltpu.SemaphoreType.DMA((6,)),
        ],
        compiler_params=pltpu.CompilerParams(
            collective_id=0, has_side_effects=True, vmem_limit_bytes=VMEM_LIMIT
        ),
        name="quantizer_backward",
    )(*(pltpu.with_memory_space_constraint(a, pltpu.HBM) for a in (tokens, cotangent, codebook, indices.reshape(1, TOK))))
    return pl.pallas_call(
        write,
        out_shape=shapes,
        in_specs=[vmem, vmem],
        out_specs=(hbm, hbm),
        scratch_shapes=[pltpu.SemaphoreType.DMA((2,))],
        compiler_params=pltpu.CompilerParams(vmem_limit_bytes=8 * 1024 * 1024),
        name="write_out",
    )(*grads)


def solution(mesh):
    return jax.shard_map(
        shards,
        mesh=mesh,
        in_specs=(P("tok", None), P("code", None), P("tok", None), P("tok")),
        out_specs=(P("tok", None), P(("code", "tok"), None)),
        check_vma=False,
    )
```

```python
import functools

import jax
import jax.numpy as jnp
from jax import lax
from jax.experimental import pallas as pl
from jax.experimental.pallas import tpu as pltpu
from jax.sharding import PartitionSpec as P

MESH = pl.DeviceIdType.MESH
F32 = jnp.float32
BF16 = jnp.bfloat16
NT = (((1,), (1,)), ((), ()))

RING = 8
FAR_FIRST = (4, 3, 5, 2, 6, 1, 7)
TOK = 1024
HALF = TOK // 2
CODES = 2048
D = 256
VMEM_LIMIT = 44 * 1024 * 1024
QUARTER = CODES // 4
ROWS = D // 2 // RING


def to_grid(row):
    return jnp.concatenate([row[:, 128 * i : 128 * (i + 1)] for i in range(HALF // 128)], axis=0)


def to_row(grid):
    return jnp.concatenate([grid[i : i + 1] for i in range(HALF // 128)], axis=1)


def combine(parts):
    top = functools.reduce(jnp.maximum, [p[0:4] for p in parts])
    total = jnp.zeros_like(top)
    weighted = jnp.zeros_like(top)
    for p in parts:
        factor = jnp.exp(p[0:4] - top)
        total = total + p[4:8] * factor
        weighted = weighted + p[8:12] * factor
    return top, total, weighted


def kernel(
    tok_hbm,
    cot_hbm,
    cb_hbm,
    idx_hbm,
    grad_tok_ref,
    grad_cb_ref,
    tok_ref,
    cot_ref,
    cb_ref,
    idx_ref,
    load_sem,
    expo,
    back,
    direct,
    cbt,
    uv_own,
    uv_other,
    uv_send,
    uv_recv,
    stat_own,
    stat_other,
    stat_1,
    stat_2,
    sum_2,
    final,
    cb_send,
    cb_recv,
    far_recv,
    cb_own,
    core_send,
    core_recv,
    ring_send,
    ring_recv,
    x_send,
    x_recv,
):
    code = lax.axis_index("code")
    x = lax.axis_index("tok")
    y, z, core = code // 16, (code // 2) % 8, code % 2
    other = (code + 1 - 2 * core, x)
    x_size = 4

    def along(axis, k):
        if axis == "z":
            return (y * 16 + ((z + k) % RING) * 2 + core, x)
        return (((y + k) % RING) * 16 + z * 2 + core, x)

    first = (("z", z), ("y", y))
    second = (("y", y), ("z", z))

    loads = [
        pltpu.make_async_copy(src, dst, load_sem.at[i])
        for i, (src, dst) in enumerate(
            ((cb_hbm, cb_ref), (tok_hbm, tok_ref), (cot_hbm, cot_ref), (idx_hbm, idx_ref))
        )
    ]
    for load in loads:
        load.start()

    barrier = pltpu.get_barrier_semaphore()

    def greet(k, carry):
        for axis in ("z", "y"):
            pl.semaphore_signal(barrier, inc=1, device_id=along(axis, k), device_id_type=MESH)
        return carry

    lax.fori_loop(1, RING, greet, 0)
    for k in (1, x_size - 1):
        pl.semaphore_signal(barrier, inc=1, device_id=(code, (x + k) % x_size), device_id_type=MESH)
    pl.semaphore_signal(barrier, inc=1, device_id=other, device_id_type=MESH)

    def ring_copy(buf, stage, half, axis, me, k, src=None):
        slot = (me + k) % RING
        return pltpu.make_async_remote_copy(
            src_ref=buf.at[half, me] if src is None else src.at[half, slot],
            dst_ref=buf.at[half, me],
            send_sem=ring_send.at[stage, half, slot],
            recv_sem=ring_recv.at[stage, half, me],
            device_id=along(axis, k),
            device_id_type=MESH,
        )

    def ring_arrival(buf, stage, half, axis, me, k):
        slot = (me + k) % RING
        return pltpu.make_async_remote_copy(
            src_ref=buf.at[half, slot],
            dst_ref=buf.at[half, slot],
            send_sem=ring_send.at[stage, half, slot],
            recv_sem=ring_recv.at[stage, half, slot],
            device_id=along(axis, k),
            device_id_type=MESH,
        )

    def ring_start(buf, stage, order, src=None, halves=(0, 1)):
        for k in FAR_FIRST:
            for half in halves:
                ring_copy(buf, stage, half, *order[half], k, src).start()

    def ring_wait(buf, stage, order):
        for k in reversed(FAR_FIRST):
            for half in range(2):
                ring_arrival(buf, stage, half, *order[half], k).wait_recv()

    def ring_drain(buf, stage, order, src=None):
        def step(k, carry):
            for half in range(2):
                ring_copy(buf, stage, half, *order[half], k, src).wait_send()
            return carry

        lax.fori_loop(1, RING, step, 0)

    def core_copy(src, dst, index):
        return pltpu.make_async_remote_copy(
            src_ref=src,
            dst_ref=dst,
            send_sem=core_send.at[index],
            recv_sem=core_recv.at[index],
            device_id=other,
            device_id_type=MESH,
        )

    def fold(value, op):
        return op(value.reshape(CODES // 8, 8, TOK), axis=0)

    loads[0].wait()
    loads[1].wait()
    logits = lax.dot_general(cb_ref[...], tok_ref[...], NT, preferred_element_type=F32)
    expo[...] = logits
    loads[2].wait()
    back[...] = lax.dot_general(cb_ref[...], cot_ref[...], NT, preferred_element_type=F32)
    top = jnp.max(fold(logits, jnp.max), axis=0, keepdims=True)
    e = jnp.exp(expo[...] - top)
    expo[...] = e
    total = jnp.sum(fold(e, jnp.sum), axis=0, keepdims=True)
    weighted = jnp.sum(fold(e * back[...], jnp.sum), axis=0, keepdims=True)

    for half in range(2):
        span = slice(half * HALF, (half + 1) * HALF)
        stat_own[half, 0:4] = to_grid(top[:, span])
        stat_own[half, 4:8] = to_grid(total[:, span])
        stat_own[half, 8:12] = to_grid(weighted[:, span])
    pl.semaphore_wait(barrier, 2 * (RING - 1) + 2 + 1)
    stat_copy = core_copy(stat_own, stat_other, 0)
    stat_copy.start()

    cbt[...] = cb_ref[...].T
    stat_copy.wait()

    scale, mean = [], []
    for half in range(2):
        states = [jnp.where(core == 0, a, b) for a, b in ((stat_own[half], stat_other[half]), (stat_other[half], stat_own[half]))]
        pair_top, pair_total, pair_weighted = combine(states)
        me = first[half][1]
        stat_1[half, me, 0:4] = pair_top
        stat_1[half, me, 4:8] = pair_total
        stat_1[half, me, 8:12] = pair_weighted
        scale.append(to_row(jnp.exp(stat_own[half, 0:4] - pair_top)))
        mean.append(to_row(pair_weighted / pair_total))
    ring_start(stat_1, 0, first)

    uv_copies = [core_copy(uv_own.at[half, 1 - core], uv_other.at[half], 1 + half) for half in range(2)]

    for half in range(2):
        span = slice(half * HALF, (half + 1) * HALF)
        e = expo[:, span] * scale[half]
        u = (e * (back[:, span] - mean[half])).astype(BF16)
        for which, weight in ((0, u), (1, e.astype(BF16))):
            value = jnp.dot(cbt[...], weight, preferred_element_type=F32).astype(BF16)
            for c in range(2):
                uv_own[half, c, which] = value[c * 128 : (c + 1) * 128]
        uv_copies[half].start()

    def uv_ring(half):
        uv_copies[half].wait()
        me = first[half][1]
        for which in range(2):
            both = uv_own[half, core, which].astype(F32) + uv_other[half, which].astype(F32)
            for k in range(RING):
                uv_send[half, k, which] = both[k * ROWS : (k + 1) * ROWS].astype(BF16)
        uv_recv[half, me] = uv_send[half, me]
        ring_start(uv_recv, 1, first, uv_send, (half,))

    uv_ring(0)

    ring_wait(stat_1, 0, first)
    for half in range(2):
        ring_top, ring_total, ring_weighted = combine([stat_1[half, j] for j in range(RING)])
        me = second[half][1]
        stat_2[half, me, 0:4] = ring_top
        stat_2[half, me, 4:8] = ring_total
        stat_2[half, me, 8:12] = ring_weighted
    ring_start(stat_2, 2, second)
    uv_ring(1)

    loads[3].wait()
    hot = lax.broadcasted_iota(jnp.int32, (CODES, TOK), 0) == idx_ref[...] - code * CODES
    hot = jnp.where(hot, 1.0, 0.0).astype(BF16)
    direct[...] = jnp.dot(hot, cot_ref[...], preferred_element_type=F32)

    ring_wait(stat_2, 2, second)
    state = [combine([stat_2[half, j] for j in range(RING)]) for half in range(2)]
    ratio = [w / t for _, t, w in state]
    local_scale = jnp.concatenate(
        [to_row(jnp.exp(stat_own[half, 0:4] - state[half][0]) / state[half][1]) for half in range(2)], axis=1
    )
    ratio_row = jnp.concatenate([to_row(ratio[half]) for half in range(2)], axis=1)

    low, high = pl.ds(0, QUARTER // 2), pl.ds(QUARTER // 2, QUARTER // 2)

    def x_copy(src, dst, index, side):
        return pltpu.make_async_remote_copy(
            src_ref=src,
            dst_ref=dst,
            send_sem=x_send.at[index],
            recv_sem=x_recv.at[index],
            device_id=(code, (x + (1, x_size - 1)[side]) % x_size),
            device_id_type=MESH,
        )

    far_copies = [x_copy(cb_send.at[2, part], far_recv.at[side], side, side) for side, part in ((0, low), (1, high))]
    near_copies = [
        x_copy(cb_send.at[side, part], cb_recv.at[side, part], 2 + side, side) for side, part in ((0, high), (1, low))
    ]
    sum_copies = [
        x_copy(cb_send.at[side, part], cb_recv.at[side, part], 4 + side, side) for side, part in ((0, low), (1, high))
    ]

    def code_rows(k):
        rows = pl.ds(pl.multiple_of(((x + k) % x_size) * QUARTER, QUARTER), QUARTER)
        grad = (expo[rows] * local_scale * (back[rows] - ratio_row)).astype(BF16)
        return jnp.dot(grad, tok_ref[...], preferred_element_type=F32) + direct[rows]

    cb_send[2] = code_rows(2).astype(BF16)
    for copy in far_copies:
        copy.start()

    ring_wait(uv_recv, 1, first)
    for half in range(2):
        acc = jnp.zeros((ROWS, HALF), F32)
        for j in range(RING):
            peer = stat_1[half, j]
            factor = jnp.exp(peer[0:4] - state[half][0]) / state[half][1]
            shift = peer[8:12] / peer[4:8] - ratio[half]
            acc = acc + to_row(factor) * (
                uv_recv[half, j, 0].astype(F32) + to_row(shift) * uv_recv[half, j, 1].astype(F32)
            )
        sum_2[half, second[half][1]] = acc.astype(BF16)
    ring_start(sum_2, 3, second)

    mid = QUARTER // 2
    part = code_rows(1)
    cb_send[0, high] = part[mid:].astype(BF16)
    near_copies[0].start()
    cb_own[0] = part[:mid]
    part = code_rows(3)
    cb_send[1, low] = part[:mid].astype(BF16)
    near_copies[1].start()
    cb_own[1] = part[mid:]
    grad_cb_ref[...] = code_rows(0)

    ring_wait(sum_2, 3, second)
    for half in range(2):
        acc = functools.reduce(jnp.add, [sum_2[half, j].astype(F32) for j in range(RING)])
        final[core, half, first[half][1]] = acc.astype(BF16)

    def final_copy(half, k):
        axis, me = first[half]
        slot = (me + k) % RING
        return pltpu.make_async_remote_copy(
            src_ref=final.at[core, half, me],
            dst_ref=final.at[core, half, me],
            send_sem=ring_send.at[4, half, slot],
            recv_sem=ring_recv.at[4, half, me],
            device_id=along(axis, k),
            device_id_type=MESH,
        )

    def final_arrival(half, k):
        axis, me = first[half]
        slot = (me + k) % RING
        return pltpu.make_async_remote_copy(
            src_ref=final.at[core, half, slot],
            dst_ref=final.at[core, half, slot],
            send_sem=ring_send.at[4, half, slot],
            recv_sem=ring_recv.at[4, half, slot],
            device_id=along(axis, k),
            device_id_type=MESH,
        )

    def final_forward(half, slot, whose):
        return core_copy(final.at[whose, half, slot], final.at[whose, half, slot], 3 + half * RING + slot)

    for k in FAR_FIRST:
        for half in range(2):
            final_copy(half, k).start()
    for half in range(2):
        final_forward(half, first[half][1], core).start()
    for side, part in ((0, low), (1, high)):
        far_copies[side].wait_recv()
        cb_send[side, part] = (cb_own[side] + far_recv[side].astype(F32)).astype(BF16)
        sum_copies[side].start()
    for k in reversed(FAR_FIRST):
        for half in range(2):
            final_arrival(half, k).wait_recv()
            final_forward(half, (first[half][1] + k) % RING, core).start()

    for copy in near_copies + sum_copies:
        copy.wait_recv()
    grad_cb_ref[...] += cb_recv[0].astype(F32) + cb_recv[1].astype(F32)

    def final_end(k, carry):
        for half in range(2):
            final_forward(half, k, 1 - core).wait_recv()
            final_forward(half, k, core).wait_send()
        return carry

    lax.fori_loop(0, RING, final_end, 0)
    for half in range(2):
        for c in range(2):
            block = jnp.concatenate([final[c, half, j].astype(F32) for j in range(RING)], axis=0)
            grad_tok_ref[half * HALF : (half + 1) * HALF, c * 128 : (c + 1) * 128] = block.T

    ring_drain(stat_1, 0, first)
    ring_drain(uv_recv, 1, first, uv_send)
    ring_drain(stat_2, 2, second)
    ring_drain(sum_2, 3, second)

    def final_drain(k, carry):
        for half in range(2):
            final_copy(half, k).wait_send()
        return carry

    lax.fori_loop(1, RING, final_drain, 0)
    for copy in far_copies + near_copies + sum_copies:
        copy.wait_send()


def write(grad_tok_ref, grad_cb_ref, tok_out, cb_out, sems):
    copies = [
        pltpu.make_async_copy(grad_tok_ref, tok_out, sems.at[0]),
        pltpu.make_async_copy(grad_cb_ref, cb_out, sems.at[1]),
    ]
    for copy in copies:
        copy.start()
    for copy in copies:
        copy.wait()


def shards(tokens, codebook, cotangent, indices):
    vmem = pl.BlockSpec(memory_space=pltpu.VMEM)
    hbm = pl.BlockSpec(memory_space=pltpu.HBM)
    shapes = (
        jax.ShapeDtypeStruct((TOK, D), F32),
        jax.ShapeDtypeStruct((QUARTER, D), F32),
    )
    grads = pl.pallas_call(
        kernel,
        out_shape=shapes,
        in_specs=[hbm] * 4,
        out_specs=(vmem, vmem),
        scratch_shapes=[
            pltpu.VMEM((TOK, D), BF16),
            pltpu.VMEM((TOK, D), BF16),
            pltpu.VMEM((CODES, D), BF16),
            pltpu.VMEM((1, TOK), jnp.int32),
            pltpu.SemaphoreType.DMA((4,)),
            pltpu.VMEM((CODES, TOK), F32),
            pltpu.VMEM((CODES, TOK), F32),
            pltpu.VMEM((CODES, D), F32),
            pltpu.VMEM((D, CODES), BF16),
            pltpu.VMEM((2, 2, 2, 128, HALF), BF16),
            pltpu.VMEM((2, 2, 128, HALF), BF16),
            pltpu.VMEM((2, RING, 2, ROWS, HALF), BF16),
            pltpu.VMEM((2, RING, 2, ROWS, HALF), BF16),
            pltpu.VMEM((2, 12, 128), F32),
            pltpu.VMEM((2, 12, 128), F32),
            pltpu.VMEM((2, RING, 12, 128), F32),
            pltpu.VMEM((2, RING, 12, 128), F32),
            pltpu.VMEM((2, RING, ROWS, HALF), BF16),
            pltpu.VMEM((2, 2, RING, ROWS, HALF), BF16),
            pltpu.VMEM((3, QUARTER, D), BF16),
            pltpu.VMEM((2, QUARTER, D), BF16),
            pltpu.VMEM((2, QUARTER // 2, D), BF16),
            pltpu.VMEM((2, QUARTER // 2, D), F32),
            pltpu.SemaphoreType.DMA((3 + 2 * RING,)),
            pltpu.SemaphoreType.DMA((3 + 2 * RING,)),
            pltpu.SemaphoreType.DMA((5, 2, RING)),
            pltpu.SemaphoreType.DMA((5, 2, RING)),
            pltpu.SemaphoreType.DMA((6,)),
            pltpu.SemaphoreType.DMA((6,)),
        ],
        compiler_params=pltpu.CompilerParams(
            collective_id=0, has_side_effects=True, vmem_limit_bytes=VMEM_LIMIT
        ),
        name="quantizer_backward",
    )(*(pltpu.with_memory_space_constraint(a, pltpu.HBM) for a in (tokens, cotangent, codebook, indices.reshape(1, TOK))))
    return pl.pallas_call(
        write,
        out_shape=shapes,
        in_specs=[vmem, vmem],
        out_specs=(hbm, hbm),
        scratch_shapes=[pltpu.SemaphoreType.DMA((2,))],
        compiler_params=pltpu.CompilerParams(vmem_limit_bytes=8 * 1024 * 1024),
        name="write_out",
    )(*grads)


def solution(mesh):
    return jax.shard_map(
        shards,
        mesh=mesh,
        in_specs=(P("tok", None), P("code", None), P("tok", None), P("tok")),
        out_specs=(P("tok", None), P(("code", "tok"), None)),
        check_vma=False,
    )
```

```python
import functools

import jax
import jax.numpy as jnp
from jax import lax
from jax.experimental import pallas as pl
from jax.experimental.pallas import tpu as pltpu
from jax.sharding import PartitionSpec as P

MESH = pl.DeviceIdType.MESH
F32 = jnp.float32
BF16 = jnp.bfloat16
NT = (((1,), (1,)), ((), ()))

RING = 8
FAR_FIRST = (4, 3, 5, 2, 6, 1, 7)
TOK = 1024
HALF = TOK // 2
CODES = 2048
D = 256
VMEM_LIMIT = 44 * 1024 * 1024
QUARTER = CODES // 4
ROWS = D // 2 // RING


def to_grid(row):
    return jnp.concatenate([row[:, 128 * i : 128 * (i + 1)] for i in range(HALF // 128)], axis=0)


def to_row(grid):
    return jnp.concatenate([grid[i : i + 1] for i in range(HALF // 128)], axis=1)


def combine(parts):
    top = functools.reduce(jnp.maximum, [p[0:4] for p in parts])
    total = jnp.zeros_like(top)
    weighted = jnp.zeros_like(top)
    for p in parts:
        factor = jnp.exp(p[0:4] - top)
        total = total + p[4:8] * factor
        weighted = weighted + p[8:12] * factor
    return top, total, weighted


def kernel(
    tok_hbm,
    cot_hbm,
    cb_hbm,
    idx_hbm,
    grad_tok_ref,
    grad_cb_ref,
    tok_ref,
    cot_ref,
    cb_ref,
    idx_ref,
    load_sem,
    expo,
    back,
    direct,
    cbt,
    uv_own,
    uv_other,
    uv_send,
    uv_recv,
    stat_own,
    stat_other,
    stat_1,
    stat_2,
    sum_2,
    final,
    cb_send,
    cb_recv,
    far_recv,
    cb_own,
    core_send,
    core_recv,
    ring_send,
    ring_recv,
    final_recv,
    x_send,
    x_recv,
):
    code = lax.axis_index("code")
    x = lax.axis_index("tok")
    y, z, core = code // 16, (code // 2) % 8, code % 2
    other = (code + 1 - 2 * core, x)
    x_size = 4

    def along(axis, k):
        if axis == "z":
            return (y * 16 + ((z + k) % RING) * 2 + core, x)
        return (((y + k) % RING) * 16 + z * 2 + core, x)

    first = (("z", z), ("y", y))
    second = (("y", y), ("z", z))

    loads = [
        pltpu.make_async_copy(src, dst, load_sem.at[i])
        for i, (src, dst) in enumerate(
            ((cb_hbm, cb_ref), (tok_hbm, tok_ref), (cot_hbm, cot_ref), (idx_hbm, idx_ref))
        )
    ]
    for load in loads:
        load.start()

    barrier = pltpu.get_barrier_semaphore()

    def greet(k, carry):
        for axis in ("z", "y"):
            pl.semaphore_signal(barrier, inc=1, device_id=along(axis, k), device_id_type=MESH)
        return carry

    lax.fori_loop(1, RING, greet, 0)
    for k in (1, x_size - 1):
        pl.semaphore_signal(barrier, inc=1, device_id=(code, (x + k) % x_size), device_id_type=MESH)
    pl.semaphore_signal(barrier, inc=1, device_id=other, device_id_type=MESH)

    def ring_copy(buf, stage, half, axis, me, k, src=None):
        return pltpu.make_async_remote_copy(
            src_ref=buf.at[half, me] if src is None else src.at[half, (me + k) % RING],
            dst_ref=buf.at[half, me],
            send_sem=ring_send.at[stage],
            recv_sem=ring_recv.at[stage],
            device_id=along(axis, k),
            device_id_type=MESH,
        )

    def ring_start(buf, stage, order, src=None, halves=(0, 1)):
        for k in FAR_FIRST:
            for half in halves:
                ring_copy(buf, stage, half, *order[half], k, src).start()

    def ring_bytes(buf, stage):
        blocks = buf.at[:, pl.ds(0, RING - 1)]
        return pltpu.make_async_remote_copy(
            src_ref=blocks,
            dst_ref=blocks,
            send_sem=ring_send.at[stage],
            recv_sem=ring_recv.at[stage],
            device_id=other,
            device_id_type=MESH,
        )

    def core_copy(src, dst, index):
        return pltpu.make_async_remote_copy(
            src_ref=src,
            dst_ref=dst,
            send_sem=core_send.at[index],
            recv_sem=core_recv.at[index],
            device_id=other,
            device_id_type=MESH,
        )

    def fold(value, op):
        return op(value.reshape(CODES // 8, 8, TOK), axis=0)

    loads[0].wait()
    loads[1].wait()
    logits = lax.dot_general(cb_ref[...], tok_ref[...], NT, preferred_element_type=F32)
    expo[...] = logits
    loads[2].wait()
    back[...] = lax.dot_general(cb_ref[...], cot_ref[...], NT, preferred_element_type=F32)
    top = jnp.max(fold(logits, jnp.max), axis=0, keepdims=True)
    e = jnp.exp(expo[...] - top)
    expo[...] = e
    total = jnp.sum(fold(e, jnp.sum), axis=0, keepdims=True)
    weighted = jnp.sum(fold(e * back[...], jnp.sum), axis=0, keepdims=True)

    for half in range(2):
        span = slice(half * HALF, (half + 1) * HALF)
        stat_own[half, 0:4] = to_grid(top[:, span])
        stat_own[half, 4:8] = to_grid(total[:, span])
        stat_own[half, 8:12] = to_grid(weighted[:, span])
    pl.semaphore_wait(barrier, 2 * (RING - 1) + 2 + 1)
    stat_copy = core_copy(stat_own, stat_other, 0)
    stat_copy.start()

    cbt[...] = cb_ref[...].T
    stat_copy.wait()

    scale, mean = [], []
    for half in range(2):
        states = [jnp.where(core == 0, a, b) for a, b in ((stat_own[half], stat_other[half]), (stat_other[half], stat_own[half]))]
        pair_top, pair_total, pair_weighted = combine(states)
        me = first[half][1]
        stat_1[half, me, 0:4] = pair_top
        stat_1[half, me, 4:8] = pair_total
        stat_1[half, me, 8:12] = pair_weighted
        scale.append(to_row(jnp.exp(stat_own[half, 0:4] - pair_top)))
        mean.append(to_row(pair_weighted / pair_total))
    ring_start(stat_1, 0, first)

    uv_copies = [core_copy(uv_own.at[half, 1 - core], uv_other.at[half], 1 + half) for half in range(2)]

    for half in range(2):
        span = slice(half * HALF, (half + 1) * HALF)
        e = expo[:, span] * scale[half]
        u = (e * (back[:, span] - mean[half])).astype(BF16)
        for which, weight in ((0, u), (1, e.astype(BF16))):
            value = jnp.dot(cbt[...], weight, preferred_element_type=F32).astype(BF16)
            for c in range(2):
                uv_own[half, c, which] = value[c * 128 : (c + 1) * 128]
        uv_copies[half].start()

    def uv_ring(half):
        uv_copies[half].wait()
        me = first[half][1]
        for which in range(2):
            both = uv_own[half, core, which].astype(F32) + uv_other[half, which].astype(F32)
            for k in range(RING):
                uv_send[half, k, which] = both[k * ROWS : (k + 1) * ROWS].astype(BF16)
        uv_recv[half, me] = uv_send[half, me]
        ring_start(uv_recv, 1, first, uv_send, (half,))

    uv_ring(0)

    ring_bytes(stat_1, 0).wait_recv()
    for half in range(2):
        ring_top, ring_total, ring_weighted = combine([stat_1[half, j] for j in range(RING)])
        me = second[half][1]
        stat_2[half, me, 0:4] = ring_top
        stat_2[half, me, 4:8] = ring_total
        stat_2[half, me, 8:12] = ring_weighted
    ring_start(stat_2, 2, second)
    uv_ring(1)

    loads[3].wait()
    hot = lax.broadcasted_iota(jnp.int32, (CODES, TOK), 0) == idx_ref[...] - code * CODES
    hot = jnp.where(hot, 1.0, 0.0).astype(BF16)
    direct[...] = jnp.dot(hot, cot_ref[...], preferred_element_type=F32)

    ring_bytes(stat_2, 2).wait_recv()
    state = [combine([stat_2[half, j] for j in range(RING)]) for half in range(2)]
    ratio = [w / t for _, t, w in state]
    local_scale = jnp.concatenate(
        [to_row(jnp.exp(stat_own[half, 0:4] - state[half][0]) / state[half][1]) for half in range(2)], axis=1
    )
    ratio_row = jnp.concatenate([to_row(ratio[half]) for half in range(2)], axis=1)

    low, high = pl.ds(0, QUARTER // 2), pl.ds(QUARTER // 2, QUARTER // 2)

    def x_copy(src, dst, send, recv, side):
        return pltpu.make_async_remote_copy(
            src_ref=src,
            dst_ref=dst,
            send_sem=x_send.at[send],
            recv_sem=x_recv.at[recv],
            device_id=(code, (x + (1, x_size - 1)[side]) % x_size),
            device_id_type=MESH,
        )

    far_copies = [x_copy(cb_send.at[2, part], far_recv.at[side], 0, side, side) for side, part in ((0, low), (1, high))]
    near_copies = [
        x_copy(cb_send.at[side, part], cb_recv.at[side, part], 1, 2, side) for side, part in ((0, high), (1, low))
    ]
    sum_copies = [
        x_copy(cb_send.at[side, part], cb_recv.at[side, part], 1, 2, side) for side, part in ((0, low), (1, high))
    ]

    def code_rows(k):
        rows = pl.ds(pl.multiple_of(((x + k) % x_size) * QUARTER, QUARTER), QUARTER)
        grad = (expo[rows] * local_scale * (back[rows] - ratio_row)).astype(BF16)
        return jnp.dot(grad, tok_ref[...], preferred_element_type=F32) + direct[rows]

    cb_send[2] = code_rows(2).astype(BF16)
    for copy in far_copies:
        copy.start()

    ring_bytes(uv_recv, 1).wait_recv()
    for half in range(2):
        acc = jnp.zeros((ROWS, HALF), F32)
        for j in range(RING):
            peer = stat_1[half, j]
            factor = jnp.exp(peer[0:4] - state[half][0]) / state[half][1]
            shift = peer[8:12] / peer[4:8] - ratio[half]
            acc = acc + to_row(factor) * (
                uv_recv[half, j, 0].astype(F32) + to_row(shift) * uv_recv[half, j, 1].astype(F32)
            )
        sum_2[half, second[half][1]] = acc.astype(BF16)
    ring_start(sum_2, 3, second)

    mid = QUARTER // 2
    part = code_rows(1)
    cb_send[0, high] = part[mid:].astype(BF16)
    near_copies[0].start()
    cb_own[0] = part[:mid]
    part = code_rows(3)
    cb_send[1, low] = part[:mid].astype(BF16)
    near_copies[1].start()
    cb_own[1] = part[mid:]
    grad_cb_ref[...] = code_rows(0)

    ring_bytes(sum_2, 3).wait_recv()
    for half in range(2):
        acc = functools.reduce(jnp.add, [sum_2[half, j].astype(F32) for j in range(RING)])
        final[core, half, first[half][1]] = acc.astype(BF16)

    def final_copy(half, k, slot):
        axis, me = first[half]
        return pltpu.make_async_remote_copy(
            src_ref=final.at[core, half, slot],
            dst_ref=final.at[core, half, slot],
            send_sem=ring_send.at[4],
            recv_sem=final_recv.at[half, slot],
            device_id=along(axis, k),
            device_id_type=MESH,
        )

    def final_forward(half, slot):
        return core_copy(final.at[core, half, slot], final.at[core, half, slot], 3)

    for k in FAR_FIRST:
        for half in range(2):
            final_copy(half, k, first[half][1]).start()
    for half in range(2):
        final_forward(half, first[half][1]).start()
    for side, part in ((0, low), (1, high)):
        far_copies[side].wait_recv()
        cb_send[side, part] = (cb_own[side] + far_recv[side].astype(F32)).astype(BF16)
        sum_copies[side].start()
    for k in reversed(FAR_FIRST):
        for half in range(2):
            slot = (first[half][1] + k) % RING
            final_copy(half, k, slot).wait_recv()
            final_forward(half, slot).start()

    x_copy(cb_send.at[pl.ds(0, 2)], cb_recv, 1, 2, 0).wait_recv()
    grad_cb_ref[...] += cb_recv[0].astype(F32) + cb_recv[1].astype(F32)

    core_copy(final.at[core], final.at[1 - core], 3).wait()
    for half in range(2):
        for c in range(2):
            block = jnp.concatenate([final[c, half, j].astype(F32) for j in range(RING)], axis=0)
            grad_tok_ref[half * HALF : (half + 1) * HALF, c * 128 : (c + 1) * 128] = block.T

    ring_bytes(stat_1, 0).wait_send()
    ring_bytes(uv_send, 1).wait_send()
    ring_bytes(stat_2, 2).wait_send()
    ring_bytes(sum_2, 3).wait_send()

    ring_bytes(final.at[core], 4).wait_send()
    x_copy(cb_send.at[2], cb_send.at[2], 0, 0, 0).wait_send()
    x_copy(cb_send.at[pl.ds(0, 2)], cb_recv, 1, 2, 0).wait_send()


def write(grad_tok_ref, grad_cb_ref, tok_out, cb_out, sems):
    copies = [
        pltpu.make_async_copy(grad_tok_ref, tok_out, sems.at[0]),
        pltpu.make_async_copy(grad_cb_ref, cb_out, sems.at[1]),
    ]
    for copy in copies:
        copy.start()
    for copy in copies:
        copy.wait()


def shards(tokens, codebook, cotangent, indices):
    vmem = pl.BlockSpec(memory_space=pltpu.VMEM)
    hbm = pl.BlockSpec(memory_space=pltpu.HBM)
    shapes = (
        jax.ShapeDtypeStruct((TOK, D), F32),
        jax.ShapeDtypeStruct((QUARTER, D), F32),
    )
    grads = pl.pallas_call(
        kernel,
        out_shape=shapes,
        in_specs=[hbm] * 4,
        out_specs=(vmem, vmem),
        scratch_shapes=[
            pltpu.VMEM((TOK, D), BF16),
            pltpu.VMEM((TOK, D), BF16),
            pltpu.VMEM((CODES, D), BF16),
            pltpu.VMEM((1, TOK), jnp.int32),
            pltpu.SemaphoreType.DMA((4,)),
            pltpu.VMEM((CODES, TOK), F32),
            pltpu.VMEM((CODES, TOK), F32),
            pltpu.VMEM((CODES, D), F32),
            pltpu.VMEM((D, CODES), BF16),
            pltpu.VMEM((2, 2, 2, 128, HALF), BF16),
            pltpu.VMEM((2, 2, 128, HALF), BF16),
            pltpu.VMEM((2, RING, 2, ROWS, HALF), BF16),
            pltpu.VMEM((2, RING, 2, ROWS, HALF), BF16),
            pltpu.VMEM((2, 12, 128), F32),
            pltpu.VMEM((2, 12, 128), F32),
            pltpu.VMEM((2, RING, 12, 128), F32),
            pltpu.VMEM((2, RING, 12, 128), F32),
            pltpu.VMEM((2, RING, ROWS, HALF), BF16),
            pltpu.VMEM((2, 2, RING, ROWS, HALF), BF16),
            pltpu.VMEM((3, QUARTER, D), BF16),
            pltpu.VMEM((2, QUARTER, D), BF16),
            pltpu.VMEM((2, QUARTER // 2, D), BF16),
            pltpu.VMEM((2, QUARTER // 2, D), F32),
            pltpu.SemaphoreType.DMA((4,)),
            pltpu.SemaphoreType.DMA((4,)),
            pltpu.SemaphoreType.DMA((5,)),
            pltpu.SemaphoreType.DMA((4,)),
            pltpu.SemaphoreType.DMA((2, RING)),
            pltpu.SemaphoreType.DMA((2,)),
            pltpu.SemaphoreType.DMA((3,)),
        ],
        compiler_params=pltpu.CompilerParams(
            collective_id=0, has_side_effects=True, vmem_limit_bytes=VMEM_LIMIT
        ),
        name="quantizer_backward",
    )(*(pltpu.with_memory_space_constraint(a, pltpu.HBM) for a in (tokens, cotangent, codebook, indices.reshape(1, TOK))))
    return pl.pallas_call(
        write,
        out_shape=shapes,
        in_specs=[vmem, vmem],
        out_specs=(hbm, hbm),
        scratch_shapes=[pltpu.SemaphoreType.DMA((2,))],
        compiler_params=pltpu.CompilerParams(vmem_limit_bytes=8 * 1024 * 1024),
        name="write_out",
    )(*grads)


def solution(mesh):
    return jax.shard_map(
        shards,
        mesh=mesh,
        in_specs=(P("tok", None), P("code", None), P("tok", None), P("tok")),
        out_specs=(P("tok", None), P(("code", "tok"), None)),
        check_vma=False,
    )
```

```python
import functools

import jax
import jax.numpy as jnp
from jax import lax
from jax.experimental import pallas as pl
from jax.experimental.pallas import tpu as pltpu
from jax.sharding import PartitionSpec as P

MESH = pl.DeviceIdType.MESH
F32 = jnp.float32
BF16 = jnp.bfloat16
NT = (((1,), (1,)), ((), ()))
TN = (((0,), (0,)), ((), ()))

RING = 8
FAR_FIRST = (4, 3, 5, 2, 6, 1, 7)
TOK = 1024
SPAN = TOK // 4
HALF = TOK // 2
CODES = 2048
D = 256
VMEM_LIMIT = 44 * 1024 * 1024
QUARTER = CODES // 4
ROWS = D // 2 // RING


def to_grid(row):
    return jnp.concatenate([row[:, 128 * i : 128 * (i + 1)] for i in range(HALF // 128)], axis=0)


def to_row(grid):
    return jnp.concatenate([grid[i : i + 1] for i in range(HALF // 128)], axis=1)


def combine(parts):
    top = functools.reduce(jnp.maximum, [p[0:4] for p in parts])
    total = jnp.zeros_like(top)
    weighted = jnp.zeros_like(top)
    for p in parts:
        factor = jnp.exp(p[0:4] - top)
        total = total + p[4:8] * factor
        weighted = weighted + p[8:12] * factor
    return top, total, weighted


def kernel(
    tok_hbm,
    cot_hbm,
    cb_hbm,
    idx_hbm,
    grad_tok_ref,
    grad_cb_ref,
    tok_ref,
    cot_ref,
    cb_ref,
    idx_ref,
    load_sem,
    expo,
    back,
    direct,
    uv_first,
    uv_own,
    uv_other,
    uv_send,
    uv_recv,
    stat_own,
    stat_other,
    stat_1,
    stat_2,
    sum_2,
    final,
    cb_send,
    cb_recv,
    far_recv,
    cb_own,
    core_send,
    core_recv,
    ring_send,
    ring_recv,
    final_recv,
    x_send,
    x_recv,
):
    code = lax.axis_index("code")
    x = lax.axis_index("tok")
    y, z, core = code // 16, (code // 2) % 8, code % 2
    other = (code + 1 - 2 * core, x)
    x_size = 4

    def along(axis, k):
        if axis == "z":
            return (y * 16 + ((z + k) % RING) * 2 + core, x)
        return (((y + k) % RING) * 16 + z * 2 + core, x)

    first = (("z", z), ("y", y))
    second = (("y", y), ("z", z))

    loads = [
        pltpu.make_async_copy(src, dst, load_sem.at[i])
        for i, (src, dst) in enumerate(
            ((cb_hbm, cb_ref), (tok_hbm, tok_ref), (cot_hbm, cot_ref), (idx_hbm, idx_ref))
        )
    ]
    for load in loads:
        load.start()

    barrier = pltpu.get_barrier_semaphore()

    def greet(k, carry):
        for axis in ("z", "y"):
            pl.semaphore_signal(barrier, inc=1, device_id=along(axis, k), device_id_type=MESH)
        return carry

    lax.fori_loop(1, RING, greet, 0)
    for k in (1, x_size - 1):
        pl.semaphore_signal(barrier, inc=1, device_id=(code, (x + k) % x_size), device_id_type=MESH)
    pl.semaphore_signal(barrier, inc=1, device_id=other, device_id_type=MESH)

    def ring_copy(buf, stage, half, axis, me, k, src=None):
        return pltpu.make_async_remote_copy(
            src_ref=buf.at[half, me] if src is None else src.at[half, (me + k) % RING],
            dst_ref=buf.at[half, me],
            send_sem=ring_send.at[stage],
            recv_sem=ring_recv.at[stage],
            device_id=along(axis, k),
            device_id_type=MESH,
        )

    def ring_start(buf, stage, order, src=None, halves=(0, 1)):
        for k in FAR_FIRST:
            for half in halves:
                ring_copy(buf, stage, half, *order[half], k, src).start()

    def ring_bytes(buf, stage, half=None):
        blocks = buf.at[slice(None) if half is None else half, pl.ds(0, RING - 1)]
        return pltpu.make_async_remote_copy(
            src_ref=blocks,
            dst_ref=blocks,
            send_sem=ring_send.at[stage],
            recv_sem=ring_recv.at[stage],
            device_id=other,
            device_id_type=MESH,
        )

    def core_copy(src, dst, index):
        return pltpu.make_async_remote_copy(
            src_ref=src,
            dst_ref=dst,
            send_sem=core_send.at[index],
            recv_sem=core_recv.at[index],
            device_id=other,
            device_id_type=MESH,
        )

    def fold(value, op):
        return op(value.reshape(CODES // 8, 8, TOK), axis=0)

    loads[0].wait()
    loads[1].wait()
    logits = lax.dot_general(cb_ref[...], tok_ref[...], NT, preferred_element_type=F32)
    expo[...] = logits
    loads[2].wait()
    back[...] = lax.dot_general(cb_ref[...], cot_ref[...], NT, preferred_element_type=F32)
    top = jnp.max(fold(logits, jnp.max), axis=0, keepdims=True)
    e = jnp.exp(expo[...] - top)
    expo[...] = e
    total = jnp.sum(fold(e, jnp.sum), axis=0, keepdims=True)
    weighted = jnp.sum(fold(e * back[...], jnp.sum), axis=0, keepdims=True)
    own_mean = weighted / total

    for half in range(2):
        span = slice(half * HALF, (half + 1) * HALF)
        stat_own[half, 0:4] = to_grid(top[:, span])
        stat_own[half, 4:8] = to_grid(total[:, span])
        stat_own[half, 8:12] = to_grid(weighted[:, span])
    pl.semaphore_wait(barrier, 2 * (RING - 1) + 2 + 1)
    stat_copy = core_copy(stat_own, stat_other, 0)
    stat_copy.start()

    def uv_terms(quarter):
        span = slice(quarter * SPAN, (quarter + 1) * SPAN)
        e = expo[:, span]
        u = (e * (back[:, span] - own_mean[:, span])).astype(BF16)
        return [
            lax.dot_general(cb_ref[...], weight, TN, preferred_element_type=F32) for weight in (u, e.astype(BF16))
        ]

    uv_first[0], uv_first[1] = uv_terms(0)
    stat_copy.wait()

    scale, mean = [], []
    for half in range(2):
        states = [jnp.where(core == 0, a, b) for a, b in ((stat_own[half], stat_other[half]), (stat_other[half], stat_own[half]))]
        pair_top, pair_total, pair_weighted = combine(states)
        me = first[half][1]
        stat_1[half, me, 0:4] = pair_top
        stat_1[half, me, 4:8] = pair_total
        stat_1[half, me, 8:12] = pair_weighted
        scale.append(to_row(jnp.exp(stat_own[half, 0:4] - pair_top)))
        mean.append(to_row(pair_weighted / pair_total))
    ring_start(stat_1, 0, first)

    scale = jnp.concatenate(scale, axis=1)
    shift = own_mean - jnp.concatenate(mean, axis=1)
    uv_copies = [core_copy(uv_own.at[q, 1 - core], uv_other.at[q], 1 + q) for q in range(4)]

    def uv_chip(quarter, u, v):
        span = slice(quarter * SPAN, (quarter + 1) * SPAN)
        u = (u + shift[:, span] * v) * scale[:, span]
        v = v * scale[:, span]
        for which, value in ((0, u), (1, v)):
            for c in range(2):
                uv_own[quarter, c, which] = value[c * 128 : (c + 1) * 128].astype(BF16)
        uv_copies[quarter].start()

    def uv_sum(quarter):
        uv_copies[quarter].wait()
        half, span = quarter // 2, slice(quarter % 2 * SPAN, (quarter % 2 + 1) * SPAN)
        for which in range(2):
            both = uv_own[quarter, core, which].astype(F32) + uv_other[quarter, which].astype(F32)
            for k in range(RING):
                uv_send[half, k, which, :, span] = both[k * ROWS : (k + 1) * ROWS].astype(BF16)

    def uv_ring(half):
        me = first[half][1]
        uv_recv[half, me] = uv_send[half, me]
        ring_start(uv_recv, 1 + half, first, uv_send, (half,))

    uv_chip(0, uv_first[0], uv_first[1])
    uv_chip(1, *uv_terms(1))
    uv_chip(2, *uv_terms(2))
    uv_sum(0)
    uv_sum(1)
    uv_ring(0)
    uv_chip(3, *uv_terms(3))
    uv_sum(2)

    ring_bytes(stat_1, 0).wait_recv()
    for half in range(2):
        ring_top, ring_total, ring_weighted = combine([stat_1[half, j] for j in range(RING)])
        me = second[half][1]
        stat_2[half, me, 0:4] = ring_top
        stat_2[half, me, 4:8] = ring_total
        stat_2[half, me, 8:12] = ring_weighted
    ring_start(stat_2, 3, second)
    uv_sum(3)
    uv_ring(1)

    loads[3].wait()
    hot = lax.broadcasted_iota(jnp.int32, (CODES, TOK), 0) == idx_ref[...] - code * CODES
    hot = jnp.where(hot, 1.0, 0.0).astype(BF16)
    direct[...] = jnp.dot(hot, cot_ref[...], preferred_element_type=F32)

    ring_bytes(stat_2, 3).wait_recv()
    state = [combine([stat_2[half, j] for j in range(RING)]) for half in range(2)]
    ratio = [w / t for _, t, w in state]
    local_scale = jnp.concatenate(
        [to_row(jnp.exp(stat_own[half, 0:4] - state[half][0]) / state[half][1]) for half in range(2)], axis=1
    )
    ratio_row = jnp.concatenate([to_row(ratio[half]) for half in range(2)], axis=1)

    low, high = pl.ds(0, QUARTER // 2), pl.ds(QUARTER // 2, QUARTER // 2)

    def x_copy(src, dst, send, recv, side):
        return pltpu.make_async_remote_copy(
            src_ref=src,
            dst_ref=dst,
            send_sem=x_send.at[send],
            recv_sem=x_recv.at[recv],
            device_id=(code, (x + (1, x_size - 1)[side]) % x_size),
            device_id_type=MESH,
        )

    far_copies = [x_copy(cb_send.at[2, part], far_recv.at[side], 0, side, side) for side, part in ((0, low), (1, high))]
    near_copies = [
        x_copy(cb_send.at[side, part], cb_recv.at[side, part], 1, 2, side) for side, part in ((0, high), (1, low))
    ]
    sum_copies = [
        x_copy(cb_send.at[side, part], cb_recv.at[side, part], 1, 2, side) for side, part in ((0, low), (1, high))
    ]

    def code_rows(k):
        rows = pl.ds(pl.multiple_of(((x + k) % x_size) * QUARTER, QUARTER), QUARTER)
        grad = (expo[rows] * local_scale * (back[rows] - ratio_row)).astype(BF16)
        return jnp.dot(grad, tok_ref[...], preferred_element_type=F32) + direct[rows]

    cb_send[2] = code_rows(2).astype(BF16)
    for copy in far_copies:
        copy.start()

    for half in range(2):
        ring_bytes(uv_recv, 1 + half, half).wait_recv()
        acc = jnp.zeros((ROWS, HALF), F32)
        for j in range(RING):
            peer = stat_1[half, j]
            factor = jnp.exp(peer[0:4] - state[half][0]) / state[half][1]
            peer_shift = peer[8:12] / peer[4:8] - ratio[half]
            acc = acc + to_row(factor) * (
                uv_recv[half, j, 0].astype(F32) + to_row(peer_shift) * uv_recv[half, j, 1].astype(F32)
            )
        sum_2[half, second[half][1]] = acc.astype(BF16)
        ring_start(sum_2, 4 + half, second, None, (half,))

    mid = QUARTER // 2
    part = code_rows(1)
    cb_send[0, high] = part[mid:].astype(BF16)
    near_copies[0].start()
    cb_own[0] = part[:mid]
    part = code_rows(3)
    cb_send[1, low] = part[:mid].astype(BF16)
    near_copies[1].start()
    cb_own[1] = part[mid:]
    grad_cb_ref[...] = code_rows(0)

    def final_copy(half, k, slot):
        axis, me = first[half]
        return pltpu.make_async_remote_copy(
            src_ref=final.at[core, half, slot],
            dst_ref=final.at[core, half, slot],
            send_sem=ring_send.at[6 + half],
            recv_sem=final_recv.at[half, slot],
            device_id=along(axis, k),
            device_id_type=MESH,
        )

    def final_forward(half, slot):
        return core_copy(final.at[core, half, slot], final.at[core, half, slot], 5)

    for half in range(2):
        ring_bytes(sum_2, 4 + half, half).wait_recv()
        me = first[half][1]
        acc = functools.reduce(jnp.add, [sum_2[half, j].astype(F32) for j in range(RING)])
        final[core, half, me] = acc.astype(BF16)
        for k in FAR_FIRST:
            final_copy(half, k, me).start()
        final_forward(half, me).start()
    for side, part in ((0, low), (1, high)):
        far_copies[side].wait_recv()
        cb_send[side, part] = (cb_own[side] + far_recv[side].astype(F32)).astype(BF16)
        sum_copies[side].start()
    for k in reversed(FAR_FIRST):
        for half in range(2):
            slot = (first[half][1] + k) % RING
            final_copy(half, k, slot).wait_recv()
            final_forward(half, slot).start()

    x_copy(cb_send.at[pl.ds(0, 2)], cb_recv, 1, 2, 0).wait_recv()
    grad_cb_ref[...] += cb_recv[0].astype(F32) + cb_recv[1].astype(F32)

    core_copy(final.at[core], final.at[1 - core], 5).wait()
    for half in range(2):
        for c in range(2):
            block = jnp.concatenate([final[c, half, j].astype(F32) for j in range(RING)], axis=0)
            grad_tok_ref[half * HALF : (half + 1) * HALF, c * 128 : (c + 1) * 128] = block.T

    ring_bytes(stat_1, 0).wait_send()
    ring_bytes(stat_2, 3).wait_send()
    for half in range(2):
        ring_bytes(uv_send, 1 + half, half).wait_send()
        ring_bytes(sum_2, 4 + half, half).wait_send()
        ring_bytes(final.at[core], 6 + half, half).wait_send()
    x_copy(cb_send.at[2], cb_send.at[2], 0, 0, 0).wait_send()
    x_copy(cb_send.at[pl.ds(0, 2)], cb_recv, 1, 2, 0).wait_send()


def write(grad_tok_ref, grad_cb_ref, tok_out, cb_out, sems):
    copies = [
        pltpu.make_async_copy(grad_tok_ref, tok_out, sems.at[0]),
        pltpu.make_async_copy(grad_cb_ref, cb_out, sems.at[1]),
    ]
    for copy in copies:
        copy.start()
    for copy in copies:
        copy.wait()


def shards(tokens, codebook, cotangent, indices):
    vmem = pl.BlockSpec(memory_space=pltpu.VMEM)
    hbm = pl.BlockSpec(memory_space=pltpu.HBM)
    shapes = (
        jax.ShapeDtypeStruct((TOK, D), F32),
        jax.ShapeDtypeStruct((QUARTER, D), F32),
    )
    grads = pl.pallas_call(
        kernel,
        out_shape=shapes,
        in_specs=[hbm] * 4,
        out_specs=(vmem, vmem),
        scratch_shapes=[
            pltpu.VMEM((TOK, D), BF16),
            pltpu.VMEM((TOK, D), BF16),
            pltpu.VMEM((CODES, D), BF16),
            pltpu.VMEM((1, TOK), jnp.int32),
            pltpu.SemaphoreType.DMA((4,)),
            pltpu.VMEM((CODES, TOK), F32),
            pltpu.VMEM((CODES, TOK), F32),
            pltpu.VMEM((CODES, D), F32),
            pltpu.VMEM((2, D, SPAN), F32),
            pltpu.VMEM((4, 2, 2, 128, SPAN), BF16),
            pltpu.VMEM((4, 2, 128, SPAN), BF16),
            pltpu.VMEM((2, RING, 2, ROWS, HALF), BF16),
            pltpu.VMEM((2, RING, 2, ROWS, HALF), BF16),
            pltpu.VMEM((2, 12, 128), F32),
            pltpu.VMEM((2, 12, 128), F32),
            pltpu.VMEM((2, RING, 12, 128), F32),
            pltpu.VMEM((2, RING, 12, 128), F32),
            pltpu.VMEM((2, RING, ROWS, HALF), BF16),
            pltpu.VMEM((2, 2, RING, ROWS, HALF), BF16),
            pltpu.VMEM((3, QUARTER, D), BF16),
            pltpu.VMEM((2, QUARTER, D), BF16),
            pltpu.VMEM((2, QUARTER // 2, D), BF16),
            pltpu.VMEM((2, QUARTER // 2, D), F32),
            pltpu.SemaphoreType.DMA((6,)),
            pltpu.SemaphoreType.DMA((6,)),
            pltpu.SemaphoreType.DMA((8,)),
            pltpu.SemaphoreType.DMA((6,)),
            pltpu.SemaphoreType.DMA((2, RING)),
            pltpu.SemaphoreType.DMA((2,)),
            pltpu.SemaphoreType.DMA((3,)),
        ],
        compiler_params=pltpu.CompilerParams(
            collective_id=0, has_side_effects=True, vmem_limit_bytes=VMEM_LIMIT
        ),
        name="quantizer_backward",
    )(*(pltpu.with_memory_space_constraint(a, pltpu.HBM) for a in (tokens, cotangent, codebook, indices.reshape(1, TOK))))
    return pl.pallas_call(
        write,
        out_shape=shapes,
        in_specs=[vmem, vmem],
        out_specs=(hbm, hbm),
        scratch_shapes=[pltpu.SemaphoreType.DMA((2,))],
        compiler_params=pltpu.CompilerParams(vmem_limit_bytes=8 * 1024 * 1024),
        name="write_out",
    )(*grads)


def solution(mesh):
    return jax.shard_map(
        shards,
        mesh=mesh,
        in_specs=(P("tok", None), P("code", None), P("tok", None), P("tok")),
        out_specs=(P("tok", None), P(("code", "tok"), None)),
        check_vma=False,
    )
```

```python
import functools

import jax
import jax.numpy as jnp
from jax import lax
from jax.experimental import pallas as pl
from jax.experimental.pallas import tpu as pltpu
from jax.sharding import PartitionSpec as P

MESH = pl.DeviceIdType.MESH
F32 = jnp.float32
BF16 = jnp.bfloat16
NT = (((1,), (1,)), ((), ()))

RING = 8
FAR_FIRST = (4, 3, 5, 2, 6, 1, 7)
TOK = 1024
HALF = TOK // 2
CODES = 2048
D = 256
VMEM_LIMIT = 44 * 1024 * 1024
QUARTER = CODES // 4
ROWS = D // 2 // RING


def to_grid(row):
    return jnp.concatenate([row[:, 128 * i : 128 * (i + 1)] for i in range(HALF // 128)], axis=0)


def to_row(grid):
    return jnp.concatenate([grid[i : i + 1] for i in range(HALF // 128)], axis=1)


def combine(parts):
    top = functools.reduce(jnp.maximum, [p[0:4] for p in parts])
    total = jnp.zeros_like(top)
    weighted = jnp.zeros_like(top)
    for p in parts:
        factor = jnp.exp(p[0:4] - top)
        total = total + p[4:8] * factor
        weighted = weighted + p[8:12] * factor
    return top, total, weighted


def kernel(
    tok_hbm,
    cot_hbm,
    cb_hbm,
    idx_hbm,
    grad_tok_ref,
    grad_cb_ref,
    tok_ref,
    cot_ref,
    cb_ref,
    idx_ref,
    load_sem,
    expo,
    back,
    direct,
    cbt,
    v_first,
    uv_own,
    uv_other,
    uv_send,
    uv_recv,
    stat_own,
    stat_other,
    stat_1,
    stat_2,
    sum_2,
    final,
    cb_send,
    cb_recv,
    far_recv,
    cb_own,
    core_send,
    core_recv,
    ring_send,
    ring_recv,
    final_recv,
    x_send,
    x_recv,
):
    code = lax.axis_index("code")
    x = lax.axis_index("tok")
    y, z, core = code // 16, (code // 2) % 8, code % 2
    other = (code + 1 - 2 * core, x)
    x_size = 4

    def along(axis, k):
        if axis == "z":
            return (y * 16 + ((z + k) % RING) * 2 + core, x)
        return (((y + k) % RING) * 16 + z * 2 + core, x)

    first = (("z", z), ("y", y))
    second = (("y", y), ("z", z))

    loads = [
        pltpu.make_async_copy(src, dst, load_sem.at[i])
        for i, (src, dst) in enumerate(
            ((cb_hbm, cb_ref), (tok_hbm, tok_ref), (cot_hbm, cot_ref), (idx_hbm, idx_ref))
        )
    ]
    for load in loads:
        load.start()

    barrier = pltpu.get_barrier_semaphore()

    def greet(k, carry):
        for axis in ("z", "y"):
            pl.semaphore_signal(barrier, inc=1, device_id=along(axis, k), device_id_type=MESH)
        return carry

    lax.fori_loop(1, RING, greet, 0)
    for k in (1, x_size - 1):
        pl.semaphore_signal(barrier, inc=1, device_id=(code, (x + k) % x_size), device_id_type=MESH)
    pl.semaphore_signal(barrier, inc=1, device_id=other, device_id_type=MESH)

    def ring_copy(buf, stage, half, axis, me, k, src=None):
        return pltpu.make_async_remote_copy(
            src_ref=buf.at[half, me] if src is None else src.at[half, (me + k) % RING],
            dst_ref=buf.at[half, me],
            send_sem=ring_send.at[stage],
            recv_sem=ring_recv.at[stage],
            device_id=along(axis, k),
            device_id_type=MESH,
        )

    def ring_start(buf, stage, order, src=None, halves=(0, 1)):
        for k in FAR_FIRST:
            for half in halves:
                ring_copy(buf, stage, half, *order[half], k, src).start()

    def ring_bytes(buf, stage):
        blocks = buf.at[:, pl.ds(0, RING - 1)]
        return pltpu.make_async_remote_copy(
            src_ref=blocks,
            dst_ref=blocks,
            send_sem=ring_send.at[stage],
            recv_sem=ring_recv.at[stage],
            device_id=other,
            device_id_type=MESH,
        )

    def core_copy(src, dst, index):
        return pltpu.make_async_remote_copy(
            src_ref=src,
            dst_ref=dst,
            send_sem=core_send.at[index],
            recv_sem=core_recv.at[index],
            device_id=other,
            device_id_type=MESH,
        )

    def fold(value, op):
        return op(value.reshape(CODES // 8, 8, TOK), axis=0)

    loads[0].wait()
    loads[1].wait()
    logits = lax.dot_general(cb_ref[...], tok_ref[...], NT, preferred_element_type=F32)
    expo[...] = logits
    loads[2].wait()
    back[...] = lax.dot_general(cb_ref[...], cot_ref[...], NT, preferred_element_type=F32)
    top = jnp.max(fold(logits, jnp.max), axis=0, keepdims=True)
    e = jnp.exp(expo[...] - top)
    expo[...] = e
    total = jnp.sum(fold(e, jnp.sum), axis=0, keepdims=True)
    weighted = jnp.sum(fold(e * back[...], jnp.sum), axis=0, keepdims=True)

    for half in range(2):
        span = slice(half * HALF, (half + 1) * HALF)
        stat_own[half, 0:4] = to_grid(top[:, span])
        stat_own[half, 4:8] = to_grid(total[:, span])
        stat_own[half, 8:12] = to_grid(weighted[:, span])
    pl.semaphore_wait(barrier, 2 * (RING - 1) + 2 + 1)
    stat_copy = core_copy(stat_own, stat_other, 0)
    stat_copy.start()

    eye = lax.broadcasted_iota(jnp.int32, (D, D), 0) == lax.broadcasted_iota(jnp.int32, (D, D), 1)
    eye = jnp.where(eye, 1.0, 0.0).astype(BF16)
    cbt[...] = lax.dot_general(eye, cb_ref[...], NT, preferred_element_type=F32).astype(BF16)

    def v_terms(half):
        weight = expo[:, half * HALF : (half + 1) * HALF].astype(BF16)
        return jnp.dot(cbt[...], weight, preferred_element_type=F32)

    v_first[...] = v_terms(0)
    stat_copy.wait()

    scale, mean = [], []
    for half in range(2):
        states = [jnp.where(core == 0, a, b) for a, b in ((stat_own[half], stat_other[half]), (stat_other[half], stat_own[half]))]
        pair_top, pair_total, pair_weighted = combine(states)
        me = first[half][1]
        stat_1[half, me, 0:4] = pair_top
        stat_1[half, me, 4:8] = pair_total
        stat_1[half, me, 8:12] = pair_weighted
        scale.append(to_row(jnp.exp(stat_own[half, 0:4] - pair_top)))
        mean.append(to_row(pair_weighted / pair_total))
    ring_start(stat_1, 0, first)

    uv_copies = [
        [core_copy(uv_own.at[which, half, 1 - core], uv_other.at[which, half], 1 + 2 * which + half) for half in range(2)]
        for which in range(2)
    ]

    def uv_chip(which, half, value):
        for c in range(2):
            uv_own[which, half, c] = value[c * 128 : (c + 1) * 128].astype(BF16)
        uv_copies[which][half].start()

    def u_terms(half):
        span = slice(half * HALF, (half + 1) * HALF)
        weight = (expo[:, span] * scale[half] * (back[:, span] - mean[half])).astype(BF16)
        return jnp.dot(cbt[...], weight, preferred_element_type=F32)

    def uv_sum(which, half):
        uv_copies[which][half].wait()
        both = uv_own[which, half, core].astype(F32) + uv_other[which, half].astype(F32)
        for k in range(RING):
            uv_send[which, half, k] = both[k * ROWS : (k + 1) * ROWS].astype(BF16)
        uv_recv[which, half, first[half][1]] = uv_send[which, half, first[half][1]]

    uv_chip(1, 0, v_first[...] * scale[0])
    uv_chip(1, 1, v_terms(1) * scale[1])
    uv_chip(0, 0, u_terms(0))
    uv_sum(1, 0)
    uv_sum(1, 1)
    ring_start(uv_recv.at[1], 1, first, uv_send.at[1])
    uv_chip(0, 1, u_terms(1))
    uv_sum(0, 0)

    ring_bytes(stat_1, 0).wait_recv()
    for half in range(2):
        ring_top, ring_total, ring_weighted = combine([stat_1[half, j] for j in range(RING)])
        me = second[half][1]
        stat_2[half, me, 0:4] = ring_top
        stat_2[half, me, 4:8] = ring_total
        stat_2[half, me, 8:12] = ring_weighted
    ring_start(stat_2, 2, second)
    uv_sum(0, 1)
    ring_start(uv_recv.at[0], 5, first, uv_send.at[0])

    loads[3].wait()
    hot = lax.broadcasted_iota(jnp.int32, (CODES, TOK), 0) == idx_ref[...] - code * CODES
    hot = jnp.where(hot, 1.0, 0.0).astype(BF16)
    direct[...] = jnp.dot(hot, cot_ref[...], preferred_element_type=F32)

    ring_bytes(stat_2, 2).wait_recv()
    state = [combine([stat_2[half, j] for j in range(RING)]) for half in range(2)]
    ratio = [w / t for _, t, w in state]
    local_scale = jnp.concatenate(
        [to_row(jnp.exp(stat_own[half, 0:4] - state[half][0]) / state[half][1]) for half in range(2)], axis=1
    )
    ratio_row = jnp.concatenate([to_row(ratio[half]) for half in range(2)], axis=1)

    low, high = pl.ds(0, QUARTER // 2), pl.ds(QUARTER // 2, QUARTER // 2)

    def x_copy(src, dst, send, recv, side):
        return pltpu.make_async_remote_copy(
            src_ref=src,
            dst_ref=dst,
            send_sem=x_send.at[send],
            recv_sem=x_recv.at[recv],
            device_id=(code, (x + (1, x_size - 1)[side]) % x_size),
            device_id_type=MESH,
        )

    far_copies = [x_copy(cb_send.at[2, part], far_recv.at[side], 0, side, side) for side, part in ((0, low), (1, high))]
    near_copies = [
        x_copy(cb_send.at[side, part], cb_recv.at[side, part], 1, 2, side) for side, part in ((0, high), (1, low))
    ]
    sum_copies = [
        x_copy(cb_send.at[side, part], cb_recv.at[side, part], 1, 2, side) for side, part in ((0, low), (1, high))
    ]

    def code_rows(k):
        rows = pl.ds(pl.multiple_of(((x + k) % x_size) * QUARTER, QUARTER), QUARTER)
        grad = (expo[rows] * local_scale * (back[rows] - ratio_row)).astype(BF16)
        return jnp.dot(grad, tok_ref[...], preferred_element_type=F32) + direct[rows]

    cb_send[2] = code_rows(2).astype(BF16)
    for copy in far_copies:
        copy.start()

    ring_bytes(uv_recv.at[1], 1).wait_recv()
    ring_bytes(uv_recv.at[0], 5).wait_recv()
    for half in range(2):
        acc = jnp.zeros((ROWS, HALF), F32)
        for j in range(RING):
            peer = stat_1[half, j]
            factor = jnp.exp(peer[0:4] - state[half][0]) / state[half][1]
            shift = peer[8:12] / peer[4:8] - ratio[half]
            acc = acc + to_row(factor) * (
                uv_recv[0, half, j].astype(F32) + to_row(shift) * uv_recv[1, half, j].astype(F32)
            )
        sum_2[half, second[half][1]] = acc.astype(BF16)
    ring_start(sum_2, 3, second)

    mid = QUARTER // 2
    part = code_rows(1)
    cb_send[0, high] = part[mid:].astype(BF16)
    near_copies[0].start()
    cb_own[0] = part[:mid]
    part = code_rows(3)
    cb_send[1, low] = part[:mid].astype(BF16)
    near_copies[1].start()
    cb_own[1] = part[mid:]
    grad_cb_ref[...] = code_rows(0)

    ring_bytes(sum_2, 3).wait_recv()
    for half in range(2):
        acc = functools.reduce(jnp.add, [sum_2[half, j].astype(F32) for j in range(RING)])
        final[core, half, first[half][1]] = acc.astype(BF16)

    def final_copy(half, k, slot):
        axis, me = first[half]
        return pltpu.make_async_remote_copy(
            src_ref=final.at[core, half, slot],
            dst_ref=final.at[core, half, slot],
            send_sem=ring_send.at[4],
            recv_sem=final_recv.at[half, slot],
            device_id=along(axis, k),
            device_id_type=MESH,
        )

    def final_forward(half, slot):
        return core_copy(final.at[core, half, slot], final.at[core, half, slot], 5)

    for k in FAR_FIRST:
        for half in range(2):
            final_copy(half, k, first[half][1]).start()
    for half in range(2):
        final_forward(half, first[half][1]).start()
    for side, part in ((0, low), (1, high)):
        far_copies[side].wait_recv()
        cb_send[side, part] = (cb_own[side] + far_recv[side].astype(F32)).astype(BF16)
        sum_copies[side].start()
    for k in reversed(FAR_FIRST):
        for half in range(2):
            slot = (first[half][1] + k) % RING
            final_copy(half, k, slot).wait_recv()
            final_forward(half, slot).start()

    x_copy(cb_send.at[pl.ds(0, 2)], cb_recv, 1, 2, 0).wait_recv()
    grad_cb_ref[...] += cb_recv[0].astype(F32) + cb_recv[1].astype(F32)

    core_copy(final.at[core], final.at[1 - core], 5).wait()
    for half in range(2):
        for c in range(2):
            block = jnp.concatenate([final[c, half, j].astype(F32) for j in range(RING)], axis=0)
            grad_tok_ref[half * HALF : (half + 1) * HALF, c * 128 : (c + 1) * 128] = block.T

    ring_bytes(stat_1, 0).wait_send()
    ring_bytes(uv_send.at[1], 1).wait_send()
    ring_bytes(uv_send.at[0], 5).wait_send()
    ring_bytes(stat_2, 2).wait_send()
    ring_bytes(sum_2, 3).wait_send()

    ring_bytes(final.at[core], 4).wait_send()
    x_copy(cb_send.at[2], cb_send.at[2], 0, 0, 0).wait_send()
    x_copy(cb_send.at[pl.ds(0, 2)], cb_recv, 1, 2, 0).wait_send()


def write(grad_tok_ref, grad_cb_ref, tok_out, cb_out, sems):
    copies = [
        pltpu.make_async_copy(grad_tok_ref, tok_out, sems.at[0]),
        pltpu.make_async_copy(grad_cb_ref, cb_out, sems.at[1]),
    ]
    for copy in copies:
        copy.start()
    for copy in copies:
        copy.wait()


def shards(tokens, codebook, cotangent, indices):
    vmem = pl.BlockSpec(memory_space=pltpu.VMEM)
    hbm = pl.BlockSpec(memory_space=pltpu.HBM)
    shapes = (
        jax.ShapeDtypeStruct((TOK, D), F32),
        jax.ShapeDtypeStruct((QUARTER, D), F32),
    )
    grads = pl.pallas_call(
        kernel,
        out_shape=shapes,
        in_specs=[hbm] * 4,
        out_specs=(vmem, vmem),
        scratch_shapes=[
            pltpu.VMEM((TOK, D), BF16),
            pltpu.VMEM((TOK, D), BF16),
            pltpu.VMEM((CODES, D), BF16),
            pltpu.VMEM((1, TOK), jnp.int32),
            pltpu.SemaphoreType.DMA((4,)),
            pltpu.VMEM((CODES, TOK), F32),
            pltpu.VMEM((CODES, TOK), F32),
            pltpu.VMEM((CODES, D), F32),
            pltpu.VMEM((D, CODES), BF16),
            pltpu.VMEM((D, HALF), F32),
            pltpu.VMEM((2, 2, 2, 128, HALF), BF16),
            pltpu.VMEM((2, 2, 128, HALF), BF16),
            pltpu.VMEM((2, 2, RING, ROWS, HALF), BF16),
            pltpu.VMEM((2, 2, RING, ROWS, HALF), BF16),
            pltpu.VMEM((2, 12, 128), F32),
            pltpu.VMEM((2, 12, 128), F32),
            pltpu.VMEM((2, RING, 12, 128), F32),
            pltpu.VMEM((2, RING, 12, 128), F32),
            pltpu.VMEM((2, RING, ROWS, HALF), BF16),
            pltpu.VMEM((2, 2, RING, ROWS, HALF), BF16),
            pltpu.VMEM((3, QUARTER, D), BF16),
            pltpu.VMEM((2, QUARTER, D), BF16),
            pltpu.VMEM((2, QUARTER // 2, D), BF16),
            pltpu.VMEM((2, QUARTER // 2, D), F32),
            pltpu.SemaphoreType.DMA((6,)),
            pltpu.SemaphoreType.DMA((6,)),
            pltpu.SemaphoreType.DMA((6,)),
            pltpu.SemaphoreType.DMA((6,)),
            pltpu.SemaphoreType.DMA((2, RING)),
            pltpu.SemaphoreType.DMA((2,)),
            pltpu.SemaphoreType.DMA((3,)),
        ],
        compiler_params=pltpu.CompilerParams(
            collective_id=0, has_side_effects=True, vmem_limit_bytes=VMEM_LIMIT
        ),
        name="quantizer_backward",
    )(*(pltpu.with_memory_space_constraint(a, pltpu.HBM) for a in (tokens, cotangent, codebook, indices.reshape(1, TOK))))
    return pl.pallas_call(
        write,
        out_shape=shapes,
        in_specs=[vmem, vmem],
        out_specs=(hbm, hbm),
        scratch_shapes=[pltpu.SemaphoreType.DMA((2,))],
        compiler_params=pltpu.CompilerParams(vmem_limit_bytes=8 * 1024 * 1024),
        name="write_out",
    )(*grads)


def solution(mesh):
    return jax.shard_map(
        shards,
        mesh=mesh,
        in_specs=(P("tok", None), P("code", None), P("tok", None), P("tok")),
        out_specs=(P("tok", None), P(("code", "tok"), None)),
        check_vma=False,
    )
```

```python
import functools

import jax
import jax.numpy as jnp
from jax import lax
from jax.experimental import pallas as pl
from jax.experimental.pallas import tpu as pltpu
from jax.sharding import PartitionSpec as P

MESH = pl.DeviceIdType.MESH
F32 = jnp.float32
BF16 = jnp.bfloat16
NT = (((1,), (1,)), ((), ()))

RING = 8
FAR_FIRST = (4, 3, 5, 2, 6, 1, 7)
TOK = 1024
HALF = TOK // 2
CODES = 2048
D = 256
VMEM_LIMIT = 44 * 1024 * 1024
QUARTER = CODES // 4
ROWS = D // 2 // RING


def to_grid(row):
    return jnp.concatenate([row[:, 128 * i : 128 * (i + 1)] for i in range(HALF // 128)], axis=0)


def to_row(grid):
    return jnp.concatenate([grid[i : i + 1] for i in range(HALF // 128)], axis=1)


def combine(parts):
    top = functools.reduce(jnp.maximum, [p[0:4] for p in parts])
    total = jnp.zeros_like(top)
    weighted = jnp.zeros_like(top)
    for p in parts:
        factor = jnp.exp(p[0:4] - top)
        total = total + p[4:8] * factor
        weighted = weighted + p[8:12] * factor
    return top, total, weighted


def kernel(
    tok_hbm,
    cot_hbm,
    cb_hbm,
    idx_hbm,
    grad_tok_ref,
    grad_cb_ref,
    tok_ref,
    cot_ref,
    cb_ref,
    idx_ref,
    load_sem,
    expo,
    back,
    direct,
    cbt,
    v_first,
    uv_own,
    uv_other,
    uv_send,
    uv_recv,
    stat_own,
    stat_other,
    stat_1,
    stat_2,
    sum_2,
    final,
    cb_send,
    cb_recv,
    far_recv,
    cb_own,
    core_send,
    core_recv,
    ring_send,
    ring_recv,
    final_recv,
    x_send,
    x_recv,
):
    code = lax.axis_index("code")
    x = lax.axis_index("tok")
    y, z, core = code // 16, (code // 2) % 8, code % 2
    other = (code + 1 - 2 * core, x)
    x_size = 4

    def along(axis, k):
        if axis == "z":
            return (y * 16 + ((z + k) % RING) * 2 + core, x)
        return (((y + k) % RING) * 16 + z * 2 + core, x)

    first = (("z", z), ("y", y))
    second = (("y", y), ("z", z))

    loads = [
        pltpu.make_async_copy(src, dst, load_sem.at[i])
        for i, (src, dst) in enumerate(
            ((cb_hbm, cb_ref), (tok_hbm, tok_ref), (cot_hbm, cot_ref), (idx_hbm, idx_ref))
        )
    ]
    for load in loads:
        load.start()

    barrier = pltpu.get_barrier_semaphore()

    def greet(k, carry):
        for axis in ("z", "y"):
            pl.semaphore_signal(barrier, inc=1, device_id=along(axis, k), device_id_type=MESH)
        return carry

    lax.fori_loop(1, RING, greet, 0)
    for k in (1, x_size - 1):
        pl.semaphore_signal(barrier, inc=1, device_id=(code, (x + k) % x_size), device_id_type=MESH)
    pl.semaphore_signal(barrier, inc=1, device_id=other, device_id_type=MESH)

    def ring_copy(buf, stage, half, axis, me, k, src=None):
        return pltpu.make_async_remote_copy(
            src_ref=buf.at[half, me] if src is None else src.at[half, (me + k) % RING],
            dst_ref=buf.at[half, me],
            send_sem=ring_send.at[stage],
            recv_sem=ring_recv.at[stage],
            device_id=along(axis, k),
            device_id_type=MESH,
        )

    def ring_start(buf, stage, order, src=None, halves=(0, 1)):
        for k in FAR_FIRST:
            for half in halves:
                ring_copy(buf, stage, half, *order[half], k, src).start()

    def ring_bytes(buf, stage):
        blocks = buf.at[:, pl.ds(0, RING - 1)]
        return pltpu.make_async_remote_copy(
            src_ref=blocks,
            dst_ref=blocks,
            send_sem=ring_send.at[stage],
            recv_sem=ring_recv.at[stage],
            device_id=other,
            device_id_type=MESH,
        )

    def core_copy(src, dst, index):
        return pltpu.make_async_remote_copy(
            src_ref=src,
            dst_ref=dst,
            send_sem=core_send.at[index],
            recv_sem=core_recv.at[index],
            device_id=other,
            device_id_type=MESH,
        )

    def fold(value, op):
        return op(value.reshape(CODES // 8, 8, TOK), axis=0)

    loads[0].wait()
    loads[1].wait()
    logits = lax.dot_general(cb_ref[...], tok_ref[...], NT, preferred_element_type=F32)
    expo[...] = logits
    loads[2].wait()
    back[...] = lax.dot_general(cb_ref[...], cot_ref[...], NT, preferred_element_type=F32)
    top = jnp.max(fold(logits, jnp.max), axis=0, keepdims=True)
    e = jnp.exp(expo[...] - top)
    expo[...] = e
    total = jnp.sum(fold(e, jnp.sum), axis=0, keepdims=True)
    weighted = jnp.sum(fold(e * back[...], jnp.sum), axis=0, keepdims=True)

    for half in range(2):
        span = slice(half * HALF, (half + 1) * HALF)
        stat_own[half, 0:4] = to_grid(top[:, span])
        stat_own[half, 4:8] = to_grid(total[:, span])
        stat_own[half, 8:12] = to_grid(weighted[:, span])
    pl.semaphore_wait(barrier, 2 * (RING - 1) + 2 + 1)
    stat_copy = core_copy(stat_own, stat_other, 0)
    stat_copy.start()

    eye = lax.broadcasted_iota(jnp.int32, (D, D), 0) == lax.broadcasted_iota(jnp.int32, (D, D), 1)
    eye = jnp.where(eye, 1.0, 0.0).astype(BF16)
    cbt[...] = lax.dot_general(eye, cb_ref[...], NT, preferred_element_type=F32).astype(BF16)

    def v_terms(half):
        weight = expo[:, half * HALF : (half + 1) * HALF].astype(BF16)
        return jnp.dot(cbt[...], weight, preferred_element_type=F32)

    v_first[...] = v_terms(0)
    stat_copy.wait()

    scale, mean = [], []
    for half in range(2):
        states = [jnp.where(core == 0, a, b) for a, b in ((stat_own[half], stat_other[half]), (stat_other[half], stat_own[half]))]
        pair_top, pair_total, pair_weighted = combine(states)
        me = first[half][1]
        stat_1[half, me, 0:4] = pair_top
        stat_1[half, me, 4:8] = pair_total
        stat_1[half, me, 8:12] = pair_weighted
        scale.append(to_row(jnp.exp(stat_own[half, 0:4] - pair_top)))
        mean.append(to_row(pair_weighted / pair_total))
    ring_start(stat_1, 0, first)

    uv_copies = [
        [core_copy(uv_own.at[which, half, 1 - core], uv_other.at[which, half], 1 + 2 * which + half) for half in range(2)]
        for which in range(2)
    ]

    def uv_chip(which, half, value):
        for c in range(2):
            uv_own[which, half, c] = value[c * 128 : (c + 1) * 128].astype(BF16)
        uv_copies[which][half].start()

    def u_terms(half):
        span = slice(half * HALF, (half + 1) * HALF)
        weight = (expo[:, span] * scale[half] * (back[:, span] - mean[half])).astype(BF16)
        return jnp.dot(cbt[...], weight, preferred_element_type=F32)

    def uv_sum(which, half):
        uv_copies[which][half].wait()
        both = uv_own[which, half, core].astype(F32) + uv_other[which, half].astype(F32)
        for k in range(RING):
            uv_send[which, half, k] = both[k * ROWS : (k + 1) * ROWS].astype(BF16)
        uv_recv[which, half, first[half][1]] = uv_send[which, half, first[half][1]]

    uv_chip(1, 0, v_first[...] * scale[0])
    uv_chip(1, 1, v_terms(1) * scale[1])
    uv_chip(0, 0, u_terms(0))
    uv_chip(0, 1, u_terms(1))
    uv_sum(1, 0)
    uv_sum(1, 1)
    ring_start(uv_recv.at[1], 1, first, uv_send.at[1])
    uv_sum(0, 0)

    ring_bytes(stat_1, 0).wait_recv()
    for half in range(2):
        ring_top, ring_total, ring_weighted = combine([stat_1[half, j] for j in range(RING)])
        me = second[half][1]
        stat_2[half, me, 0:4] = ring_top
        stat_2[half, me, 4:8] = ring_total
        stat_2[half, me, 8:12] = ring_weighted
    ring_start(stat_2, 2, second)
    ring_start(uv_recv.at[0], 5, first, uv_send.at[0], (0,))
    uv_sum(0, 1)
    ring_start(uv_recv.at[0], 5, first, uv_send.at[0], (1,))

    loads[3].wait()
    hot = lax.broadcasted_iota(jnp.int32, (CODES, TOK), 0) == idx_ref[...] - code * CODES
    hot = jnp.where(hot, 1.0, 0.0).astype(BF16)
    direct[...] = jnp.dot(hot, cot_ref[...], preferred_element_type=F32)

    ring_bytes(stat_2, 2).wait_recv()
    state = [combine([stat_2[half, j] for j in range(RING)]) for half in range(2)]
    ratio = [w / t for _, t, w in state]
    local_scale = jnp.concatenate(
        [to_row(jnp.exp(stat_own[half, 0:4] - state[half][0]) / state[half][1]) for half in range(2)], axis=1
    )
    ratio_row = jnp.concatenate([to_row(ratio[half]) for half in range(2)], axis=1)

    low, high = pl.ds(0, QUARTER // 2), pl.ds(QUARTER // 2, QUARTER // 2)

    def x_copy(src, dst, send, recv, side):
        return pltpu.make_async_remote_copy(
            src_ref=src,
            dst_ref=dst,
            send_sem=x_send.at[send],
            recv_sem=x_recv.at[recv],
            device_id=(code, (x + (1, x_size - 1)[side]) % x_size),
            device_id_type=MESH,
        )

    far_copies = [x_copy(cb_send.at[2, part], far_recv.at[side], 0, side, side) for side, part in ((0, low), (1, high))]
    near_copies = [
        x_copy(cb_send.at[side, part], cb_recv.at[side, part], 1, 2, side) for side, part in ((0, high), (1, low))
    ]
    sum_copies = [
        x_copy(cb_send.at[side, part], cb_recv.at[side, part], 1, 2, side) for side, part in ((0, low), (1, high))
    ]

    def code_rows(k):
        rows = pl.ds(pl.multiple_of(((x + k) % x_size) * QUARTER, QUARTER), QUARTER)
        grad = (expo[rows] * local_scale * (back[rows] - ratio_row)).astype(BF16)
        return jnp.dot(grad, tok_ref[...], preferred_element_type=F32) + direct[rows]

    ring_bytes(uv_recv.at[1], 1).wait_recv()
    ring_bytes(uv_recv.at[0], 5).wait_recv()
    for half in range(2):
        acc = jnp.zeros((ROWS, HALF), F32)
        for j in range(RING):
            peer = stat_1[half, j]
            factor = jnp.exp(peer[0:4] - state[half][0]) / state[half][1]
            shift = peer[8:12] / peer[4:8] - ratio[half]
            acc = acc + to_row(factor) * (
                uv_recv[0, half, j].astype(F32) + to_row(shift) * uv_recv[1, half, j].astype(F32)
            )
        sum_2[half, second[half][1]] = acc.astype(BF16)
    ring_start(sum_2, 3, second)

    cb_send[2] = code_rows(2).astype(BF16)
    for copy in far_copies:
        copy.start()


    mid = QUARTER // 2
    part = code_rows(1)
    cb_send[0, high] = part[mid:].astype(BF16)
    near_copies[0].start()
    cb_own[0] = part[:mid]
    part = code_rows(3)
    cb_send[1, low] = part[:mid].astype(BF16)
    near_copies[1].start()
    cb_own[1] = part[mid:]
    grad_cb_ref[...] = code_rows(0)

    ring_bytes(sum_2, 3).wait_recv()
    for half in range(2):
        acc = functools.reduce(jnp.add, [sum_2[half, j].astype(F32) for j in range(RING)])
        final[core, half, first[half][1]] = acc.astype(BF16)

    def final_copy(half, k, slot):
        axis, me = first[half]
        return pltpu.make_async_remote_copy(
            src_ref=final.at[core, half, slot],
            dst_ref=final.at[core, half, slot],
            send_sem=ring_send.at[4],
            recv_sem=final_recv.at[half, slot],
            device_id=along(axis, k),
            device_id_type=MESH,
        )

    def final_forward(half, slot):
        return core_copy(final.at[core, half, slot], final.at[core, half, slot], 5)

    for k in FAR_FIRST:
        for half in range(2):
            final_copy(half, k, first[half][1]).start()
    for half in range(2):
        final_forward(half, first[half][1]).start()
    for side, part in ((0, low), (1, high)):
        far_copies[side].wait_recv()
        cb_send[side, part] = (cb_own[side] + far_recv[side].astype(F32)).astype(BF16)
        sum_copies[side].start()
    for k in reversed(FAR_FIRST):
        for half in range(2):
            slot = (first[half][1] + k) % RING
            final_copy(half, k, slot).wait_recv()
            final_forward(half, slot).start()

    def turn_rows(c):
        for half in range(2):
            block = jnp.concatenate([final[c, half, j].astype(F32) for j in range(RING)], axis=0)
            lanes = pl.ds(pl.multiple_of(c * 128, 128), 128)
            grad_tok_ref[half * HALF : (half + 1) * HALF, lanes] = block.T

    turn_rows(core)
    x_copy(cb_send.at[pl.ds(0, 2)], cb_recv, 1, 2, 0).wait_recv()
    grad_cb_ref[...] += cb_recv[0].astype(F32) + cb_recv[1].astype(F32)
    core_copy(final.at[core], final.at[1 - core], 5).wait()
    turn_rows(1 - core)

    ring_bytes(stat_1, 0).wait_send()
    ring_bytes(uv_send.at[1], 1).wait_send()
    ring_bytes(uv_send.at[0], 5).wait_send()
    ring_bytes(stat_2, 2).wait_send()
    ring_bytes(sum_2, 3).wait_send()

    ring_bytes(final.at[core], 4).wait_send()
    x_copy(cb_send.at[2], cb_send.at[2], 0, 0, 0).wait_send()
    x_copy(cb_send.at[pl.ds(0, 2)], cb_recv, 1, 2, 0).wait_send()


def write(grad_tok_ref, grad_cb_ref, tok_out, cb_out, sems):
    copies = [
        pltpu.make_async_copy(grad_tok_ref, tok_out, sems.at[0]),
        pltpu.make_async_copy(grad_cb_ref, cb_out, sems.at[1]),
    ]
    for copy in copies:
        copy.start()
    for copy in copies:
        copy.wait()


def shards(tokens, codebook, cotangent, indices):
    vmem = pl.BlockSpec(memory_space=pltpu.VMEM)
    hbm = pl.BlockSpec(memory_space=pltpu.HBM)
    shapes = (
        jax.ShapeDtypeStruct((TOK, D), F32),
        jax.ShapeDtypeStruct((QUARTER, D), F32),
    )
    grads = pl.pallas_call(
        kernel,
        out_shape=shapes,
        in_specs=[hbm] * 4,
        out_specs=(vmem, vmem),
        scratch_shapes=[
            pltpu.VMEM((TOK, D), BF16),
            pltpu.VMEM((TOK, D), BF16),
            pltpu.VMEM((CODES, D), BF16),
            pltpu.VMEM((1, TOK), jnp.int32),
            pltpu.SemaphoreType.DMA((4,)),
            pltpu.VMEM((CODES, TOK), F32),
            pltpu.VMEM((CODES, TOK), F32),
            pltpu.VMEM((CODES, D), F32),
            pltpu.VMEM((D, CODES), BF16),
            pltpu.VMEM((D, HALF), F32),
            pltpu.VMEM((2, 2, 2, 128, HALF), BF16),
            pltpu.VMEM((2, 2, 128, HALF), BF16),
            pltpu.VMEM((2, 2, RING, ROWS, HALF), BF16),
            pltpu.VMEM((2, 2, RING, ROWS, HALF), BF16),
            pltpu.VMEM((2, 12, 128), F32),
            pltpu.VMEM((2, 12, 128), F32),
            pltpu.VMEM((2, RING, 12, 128), F32),
            pltpu.VMEM((2, RING, 12, 128), F32),
            pltpu.VMEM((2, RING, ROWS, HALF), BF16),
            pltpu.VMEM((2, 2, RING, ROWS, HALF), BF16),
            pltpu.VMEM((3, QUARTER, D), BF16),
            pltpu.VMEM((2, QUARTER, D), BF16),
            pltpu.VMEM((2, QUARTER // 2, D), BF16),
            pltpu.VMEM((2, QUARTER // 2, D), F32),
            pltpu.SemaphoreType.DMA((6,)),
            pltpu.SemaphoreType.DMA((6,)),
            pltpu.SemaphoreType.DMA((6,)),
            pltpu.SemaphoreType.DMA((6,)),
            pltpu.SemaphoreType.DMA((2, RING)),
            pltpu.SemaphoreType.DMA((2,)),
            pltpu.SemaphoreType.DMA((3,)),
        ],
        compiler_params=pltpu.CompilerParams(
            collective_id=0, has_side_effects=True, vmem_limit_bytes=VMEM_LIMIT
        ),
        name="quantizer_backward",
    )(*(pltpu.with_memory_space_constraint(a, pltpu.HBM) for a in (tokens, cotangent, codebook, indices.reshape(1, TOK))))
    return pl.pallas_call(
        write,
        out_shape=shapes,
        in_specs=[vmem, vmem],
        out_specs=(hbm, hbm),
        scratch_shapes=[pltpu.SemaphoreType.DMA((2,))],
        compiler_params=pltpu.CompilerParams(vmem_limit_bytes=8 * 1024 * 1024),
        name="write_out",
    )(*grads)


def solution(mesh):
    return jax.shard_map(
        shards,
        mesh=mesh,
        in_specs=(P("tok", None), P("code", None), P("tok", None), P("tok")),
        out_specs=(P("tok", None), P(("code", "tok"), None)),
        check_vma=False,
    )
```

```python
import functools

import jax
import jax.numpy as jnp
from jax import lax
from jax.experimental import pallas as pl
from jax.experimental.pallas import tpu as pltpu
from jax.sharding import PartitionSpec as P

MESH = pl.DeviceIdType.MESH
F32 = jnp.float32
BF16 = jnp.bfloat16
NT = (((1,), (1,)), ((), ()))

RING = 8
FAR_FIRST = (4, 3, 5, 2, 6, 1, 7)
TOK = 1024
HALF = TOK // 2
CODES = 2048
D = 256
VMEM_LIMIT = 44 * 1024 * 1024
QUARTER = CODES // 4
ROWS = D // 2 // RING


def to_grid(row):
    return jnp.concatenate([row[:, 128 * i : 128 * (i + 1)] for i in range(HALF // 128)], axis=0)


def to_row(grid):
    return jnp.concatenate([grid[i : i + 1] for i in range(HALF // 128)], axis=1)


def combine(parts):
    top = functools.reduce(jnp.maximum, [p[0:4] for p in parts])
    total = jnp.zeros_like(top)
    weighted = jnp.zeros_like(top)
    for p in parts:
        factor = jnp.exp(p[0:4] - top)
        total = total + p[4:8] * factor
        weighted = weighted + p[8:12] * factor
    return top, total, weighted


def kernel(
    tok_hbm,
    cot_hbm,
    cb_hbm,
    idx_hbm,
    grad_tok_ref,
    grad_cb_ref,
    tok_ref,
    cot_ref,
    cb_ref,
    idx_ref,
    load_sem,
    expo,
    back,
    direct,
    cbt,
    v_first,
    uv_own,
    uv_other,
    uv_send,
    uv_recv,
    stat_own,
    stat_other,
    stat_1,
    stat_2,
    mix,
    sum_2,
    final,
    cb_send,
    cb_recv,
    far_recv,
    cb_own,
    core_send,
    core_recv,
    ring_send,
    ring_recv,
    final_recv,
    x_send,
    x_recv,
):
    code = lax.axis_index("code")
    x = lax.axis_index("tok")
    y, z, core = code // 16, (code // 2) % 8, code % 2
    other = (code + 1 - 2 * core, x)
    x_size = 4

    def along(axis, k):
        if axis == "z":
            return (y * 16 + ((z + k) % RING) * 2 + core, x)
        return (((y + k) % RING) * 16 + z * 2 + core, x)

    first = (("z", z), ("y", y))
    second = (("y", y), ("z", z))

    loads = [
        pltpu.make_async_copy(src, dst, load_sem.at[i])
        for i, (src, dst) in enumerate(
            ((cb_hbm, cb_ref), (tok_hbm, tok_ref), (cot_hbm, cot_ref), (idx_hbm, idx_ref))
        )
    ]
    for load in loads:
        load.start()

    barrier = pltpu.get_barrier_semaphore()

    def greet(k, carry):
        for axis in ("z", "y"):
            pl.semaphore_signal(barrier, inc=1, device_id=along(axis, k), device_id_type=MESH)
        return carry

    lax.fori_loop(1, RING, greet, 0)
    for k in (1, x_size - 1):
        pl.semaphore_signal(barrier, inc=1, device_id=(code, (x + k) % x_size), device_id_type=MESH)
    pl.semaphore_signal(barrier, inc=1, device_id=other, device_id_type=MESH)

    def ring_copy(buf, stage, half, axis, me, k, src=None):
        return pltpu.make_async_remote_copy(
            src_ref=buf.at[half, me] if src is None else src.at[half, (me + k) % RING],
            dst_ref=buf.at[half, me],
            send_sem=ring_send.at[stage],
            recv_sem=ring_recv.at[stage],
            device_id=along(axis, k),
            device_id_type=MESH,
        )

    def ring_start(buf, stage, order, src=None, halves=(0, 1)):
        for k in FAR_FIRST:
            for half in halves:
                ring_copy(buf, stage, half, *order[half], k, src).start()

    def ring_bytes(buf, stage):
        blocks = buf.at[:, pl.ds(0, RING - 1)]
        return pltpu.make_async_remote_copy(
            src_ref=blocks,
            dst_ref=blocks,
            send_sem=ring_send.at[stage],
            recv_sem=ring_recv.at[stage],
            device_id=other,
            device_id_type=MESH,
        )

    def core_copy(src, dst, index):
        return pltpu.make_async_remote_copy(
            src_ref=src,
            dst_ref=dst,
            send_sem=core_send.at[index],
            recv_sem=core_recv.at[index],
            device_id=other,
            device_id_type=MESH,
        )

    def fold(value, op):
        return op(value.reshape(CODES // 8, 8, TOK), axis=0)

    loads[0].wait()
    loads[1].wait()
    logits = lax.dot_general(cb_ref[...], tok_ref[...], NT, preferred_element_type=F32)
    expo[...] = logits
    loads[2].wait()
    back[...] = lax.dot_general(cb_ref[...], cot_ref[...], NT, preferred_element_type=F32)
    top = jnp.max(fold(logits, jnp.max), axis=0, keepdims=True)
    e = jnp.exp(expo[...] - top)
    expo[...] = e
    total = jnp.sum(fold(e, jnp.sum), axis=0, keepdims=True)
    weighted = jnp.sum(fold(e * back[...], jnp.sum), axis=0, keepdims=True)

    for half in range(2):
        span = slice(half * HALF, (half + 1) * HALF)
        stat_own[half, 0:4] = to_grid(top[:, span])
        stat_own[half, 4:8] = to_grid(total[:, span])
        stat_own[half, 8:12] = to_grid(weighted[:, span])
    pl.semaphore_wait(barrier, 2 * (RING - 1) + 2 + 1)
    stat_copy = core_copy(stat_own, stat_other, 0)
    stat_copy.start()

    eye = lax.broadcasted_iota(jnp.int32, (D, D), 0) == lax.broadcasted_iota(jnp.int32, (D, D), 1)
    eye = jnp.where(eye, 1.0, 0.0).astype(BF16)
    cbt[...] = lax.dot_general(eye, cb_ref[...], NT, preferred_element_type=F32).astype(BF16)

    def v_terms(half):
        weight = expo[:, half * HALF : (half + 1) * HALF].astype(BF16)
        return jnp.dot(cbt[...], weight, preferred_element_type=F32)

    v_first[...] = v_terms(0)
    stat_copy.wait()

    scale, mean = [], []
    for half in range(2):
        states = [jnp.where(core == 0, a, b) for a, b in ((stat_own[half], stat_other[half]), (stat_other[half], stat_own[half]))]
        pair_top, pair_total, pair_weighted = combine(states)
        me = first[half][1]
        stat_1[half, me, 0:4] = pair_top
        stat_1[half, me, 4:8] = pair_total
        stat_1[half, me, 8:12] = pair_weighted
        scale.append(to_row(jnp.exp(stat_own[half, 0:4] - pair_top)))
        mean.append(to_row(pair_weighted / pair_total))
    ring_start(stat_1, 0, first)

    uv_copies = [
        [core_copy(uv_own.at[which, half, 1 - core], uv_other.at[which, half], 1 + 2 * which + half) for half in range(2)]
        for which in range(2)
    ]

    def uv_chip(which, half, value):
        for c in range(2):
            uv_own[which, half, c] = value[c * 128 : (c + 1) * 128].astype(BF16)
        uv_copies[which][half].start()

    def u_terms(half):
        span = slice(half * HALF, (half + 1) * HALF)
        weight = (expo[:, span] * scale[half] * (back[:, span] - mean[half])).astype(BF16)
        return jnp.dot(cbt[...], weight, preferred_element_type=F32)

    def uv_sum(which, half):
        uv_copies[which][half].wait()
        both = uv_own[which, half, core].astype(F32) + uv_other[which, half].astype(F32)
        for k in range(RING):
            uv_send[which, half, k] = both[k * ROWS : (k + 1) * ROWS].astype(BF16)
        uv_recv[which, half, first[half][1]] = uv_send[which, half, first[half][1]]

    uv_chip(1, 0, v_first[...] * scale[0])
    uv_chip(1, 1, v_terms(1) * scale[1])
    uv_chip(0, 0, u_terms(0))
    uv_chip(0, 1, u_terms(1))
    uv_sum(1, 0)
    uv_sum(1, 1)
    ring_start(uv_recv.at[1], 1, first, uv_send.at[1])
    uv_sum(0, 0)

    ring_bytes(stat_1, 0).wait_recv()
    for half in range(2):
        ring_top, ring_total, ring_weighted = combine([stat_1[half, j] for j in range(RING)])
        me = second[half][1]
        stat_2[half, me, 0:4] = ring_top
        stat_2[half, me, 4:8] = ring_total
        stat_2[half, me, 8:12] = ring_weighted
    ring_start(stat_2, 2, second)
    ring_start(uv_recv.at[0], 5, first, uv_send.at[0], (0,))
    uv_sum(0, 1)
    ring_start(uv_recv.at[0], 5, first, uv_send.at[0], (1,))

    loads[3].wait()
    hot = lax.broadcasted_iota(jnp.int32, (CODES, TOK), 0) == idx_ref[...] - code * CODES
    hot = jnp.where(hot, 1.0, 0.0).astype(BF16)
    direct[...] = jnp.dot(hot, cot_ref[...], preferred_element_type=F32)

    ring_bytes(stat_2, 2).wait_recv()
    state = [combine([stat_2[half, j] for j in range(RING)]) for half in range(2)]
    ratio = [w / t for _, t, w in state]
    local_scale = jnp.concatenate(
        [to_row(jnp.exp(stat_own[half, 0:4] - state[half][0]) / state[half][1]) for half in range(2)], axis=1
    )
    ratio_row = jnp.concatenate([to_row(ratio[half]) for half in range(2)], axis=1)

    low, high = pl.ds(0, QUARTER // 2), pl.ds(QUARTER // 2, QUARTER // 2)

    def x_copy(src, dst, send, recv, side):
        return pltpu.make_async_remote_copy(
            src_ref=src,
            dst_ref=dst,
            send_sem=x_send.at[send],
            recv_sem=x_recv.at[recv],
            device_id=(code, (x + (1, x_size - 1)[side]) % x_size),
            device_id_type=MESH,
        )

    far_copies = [x_copy(cb_send.at[2, part], far_recv.at[side], 0, side, side) for side, part in ((0, low), (1, high))]
    near_copies = [
        x_copy(cb_send.at[side, part], cb_recv.at[side, part], 1, 2, side) for side, part in ((0, high), (1, low))
    ]
    sum_copies = [
        x_copy(cb_send.at[side, part], cb_recv.at[side, part], 1, 2, side) for side, part in ((0, low), (1, high))
    ]

    def code_rows(k):
        rows = pl.ds(pl.multiple_of(((x + k) % x_size) * QUARTER, QUARTER), QUARTER)
        grad = (expo[rows] * local_scale * (back[rows] - ratio_row)).astype(BF16)
        return jnp.dot(grad, tok_ref[...], preferred_element_type=F32) + direct[rows]

    for half in range(2):
        for j in range(RING):
            peer = stat_1[half, j]
            factor = jnp.exp(peer[0:4] - state[half][0]) / state[half][1]
            shift = peer[8:12] / peer[4:8] - ratio[half]
            mix[half, j, 0:1] = to_row(factor)
            mix[half, j, 1:2] = to_row(factor * shift)
    ring_bytes(uv_recv.at[1], 1).wait_recv()
    ring_bytes(uv_recv.at[0], 5).wait_recv()
    for half in range(2):
        acc = jnp.zeros((ROWS, HALF), F32)
        for j in range(RING):
            acc = acc + mix[half, j, 0:1] * uv_recv[0, half, j].astype(F32)
            acc = acc + mix[half, j, 1:2] * uv_recv[1, half, j].astype(F32)
        sum_2[half, second[half][1]] = acc.astype(BF16)
    ring_start(sum_2, 3, second)

    cb_send[2] = code_rows(2).astype(BF16)
    for copy in far_copies:
        copy.start()


    mid = QUARTER // 2
    part = code_rows(1)
    cb_send[0, high] = part[mid:].astype(BF16)
    near_copies[0].start()
    cb_own[0] = part[:mid]
    part = code_rows(3)
    cb_send[1, low] = part[:mid].astype(BF16)
    near_copies[1].start()
    cb_own[1] = part[mid:]
    grad_cb_ref[...] = code_rows(0)

    ring_bytes(sum_2, 3).wait_recv()
    for half in range(2):
        acc = functools.reduce(jnp.add, [sum_2[half, j].astype(F32) for j in range(RING)])
        final[core, half, first[half][1]] = acc.astype(BF16)

    def final_copy(half, k, slot):
        axis, me = first[half]
        return pltpu.make_async_remote_copy(
            src_ref=final.at[core, half, slot],
            dst_ref=final.at[core, half, slot],
            send_sem=ring_send.at[4],
            recv_sem=final_recv.at[k],
            device_id=along(axis, k),
            device_id_type=MESH,
        )

    def final_forward(half, slot):
        return core_copy(final.at[core, half, slot], final.at[core, half, slot], 5)

    for k in FAR_FIRST:
        for half in range(2):
            final_copy(half, k, first[half][1]).start()
    for half in range(2):
        final_forward(half, first[half][1]).start()
    for side, part in ((0, low), (1, high)):
        far_copies[side].wait_recv()
        cb_send[side, part] = (cb_own[side] + far_recv[side].astype(F32)).astype(BF16)
        sum_copies[side].start()
    for k in reversed(FAR_FIRST):
        both = final.at[core, :, 0]
        pltpu.make_async_remote_copy(
            src_ref=both,
            dst_ref=both,
            send_sem=ring_send.at[4],
            recv_sem=final_recv.at[RING - k],
            device_id=other,
            device_id_type=MESH,
        ).wait_recv()
        for half in range(2):
            final_forward(half, (first[half][1] + k) % RING).start()

    def turn_rows(c):
        for half in range(2):
            block = jnp.concatenate([final[c, half, j].astype(F32) for j in range(RING)], axis=0)
            lanes = pl.ds(pl.multiple_of(c * 128, 128), 128)
            grad_tok_ref[half * HALF : (half + 1) * HALF, lanes] = block.T

    turn_rows(core)
    x_copy(cb_send.at[pl.ds(0, 2)], cb_recv, 1, 2, 0).wait_recv()
    grad_cb_ref[...] += cb_recv[0].astype(F32) + cb_recv[1].astype(F32)
    core_copy(final.at[core], final.at[1 - core], 5).wait()
    turn_rows(1 - core)

    ring_bytes(stat_1, 0).wait_send()
    ring_bytes(uv_send.at[1], 1).wait_send()
    ring_bytes(uv_send.at[0], 5).wait_send()
    ring_bytes(stat_2, 2).wait_send()
    ring_bytes(sum_2, 3).wait_send()

    ring_bytes(final.at[core], 4).wait_send()
    x_copy(cb_send.at[2], cb_send.at[2], 0, 0, 0).wait_send()
    x_copy(cb_send.at[pl.ds(0, 2)], cb_recv, 1, 2, 0).wait_send()


def write(grad_tok_ref, grad_cb_ref, tok_out, cb_out, sems):
    copies = [
        pltpu.make_async_copy(grad_tok_ref, tok_out, sems.at[0]),
        pltpu.make_async_copy(grad_cb_ref, cb_out, sems.at[1]),
    ]
    for copy in copies:
        copy.start()
    for copy in copies:
        copy.wait()


def shards(tokens, codebook, cotangent, indices):
    vmem = pl.BlockSpec(memory_space=pltpu.VMEM)
    hbm = pl.BlockSpec(memory_space=pltpu.HBM)
    shapes = (
        jax.ShapeDtypeStruct((TOK, D), F32),
        jax.ShapeDtypeStruct((QUARTER, D), F32),
    )
    grads = pl.pallas_call(
        kernel,
        out_shape=shapes,
        in_specs=[hbm] * 4,
        out_specs=(vmem, vmem),
        scratch_shapes=[
            pltpu.VMEM((TOK, D), BF16),
            pltpu.VMEM((TOK, D), BF16),
            pltpu.VMEM((CODES, D), BF16),
            pltpu.VMEM((1, TOK), jnp.int32),
            pltpu.SemaphoreType.DMA((4,)),
            pltpu.VMEM((CODES, TOK), F32),
            pltpu.VMEM((CODES, TOK), F32),
            pltpu.VMEM((CODES, D), F32),
            pltpu.VMEM((D, CODES), BF16),
            pltpu.VMEM((D, HALF), F32),
            pltpu.VMEM((2, 2, 2, 128, HALF), BF16),
            pltpu.VMEM((2, 2, 128, HALF), BF16),
            pltpu.VMEM((2, 2, RING, ROWS, HALF), BF16),
            pltpu.VMEM((2, 2, RING, ROWS, HALF), BF16),
            pltpu.VMEM((2, 12, 128), F32),
            pltpu.VMEM((2, 12, 128), F32),
            pltpu.VMEM((2, RING, 12, 128), F32),
            pltpu.VMEM((2, RING, 12, 128), F32),
            pltpu.VMEM((2, RING, 2, HALF), F32),
            pltpu.VMEM((2, RING, ROWS, HALF), BF16),
            pltpu.VMEM((2, 2, RING, ROWS, HALF), BF16),
            pltpu.VMEM((3, QUARTER, D), BF16),
            pltpu.VMEM((2, QUARTER, D), BF16),
            pltpu.VMEM((2, QUARTER // 2, D), BF16),
            pltpu.VMEM((2, QUARTER // 2, D), F32),
            pltpu.SemaphoreType.DMA((6,)),
            pltpu.SemaphoreType.DMA((6,)),
            pltpu.SemaphoreType.DMA((6,)),
            pltpu.SemaphoreType.DMA((6,)),
            pltpu.SemaphoreType.DMA((RING,)),
            pltpu.SemaphoreType.DMA((2,)),
            pltpu.SemaphoreType.DMA((3,)),
        ],
        compiler_params=pltpu.CompilerParams(
            collective_id=0, has_side_effects=True, vmem_limit_bytes=VMEM_LIMIT
        ),
        name="quantizer_backward",
    )(*(pltpu.with_memory_space_constraint(a, pltpu.HBM) for a in (tokens, cotangent, codebook, indices.reshape(1, TOK))))
    return pl.pallas_call(
        write,
        out_shape=shapes,
        in_specs=[vmem, vmem],
        out_specs=(hbm, hbm),
        scratch_shapes=[pltpu.SemaphoreType.DMA((2,))],
        compiler_params=pltpu.CompilerParams(vmem_limit_bytes=8 * 1024 * 1024),
        name="write_out",
    )(*grads)


def solution(mesh):
    return jax.shard_map(
        shards,
        mesh=mesh,
        in_specs=(P("tok", None), P("code", None), P("tok", None), P("tok")),
        out_specs=(P("tok", None), P(("code", "tok"), None)),
        check_vma=False,
    )
```

```python
import functools

import jax
import jax.numpy as jnp
from jax import lax
from jax.experimental import pallas as pl
from jax.experimental.pallas import tpu as pltpu
from jax.sharding import PartitionSpec as P

MESH = pl.DeviceIdType.MESH
F32 = jnp.float32
BF16 = jnp.bfloat16
NT = (((1,), (1,)), ((), ()))

RING = 8
FAR_FIRST = (4, 3, 5, 2, 6, 1, 7)
TOK = 1024
HALF = TOK // 2
CODES = 2048
D = 256
VMEM_LIMIT = 44 * 1024 * 1024
QUARTER = CODES // 4
ROWS = D // 2 // RING


def to_grid(row):
    return jnp.concatenate([row[:, 128 * i : 128 * (i + 1)] for i in range(HALF // 128)], axis=0)


def to_row(grid):
    return jnp.concatenate([grid[i : i + 1] for i in range(HALF // 128)], axis=1)


def combine(parts):
    top = functools.reduce(jnp.maximum, [p[0:4] for p in parts])
    total = jnp.zeros_like(top)
    weighted = jnp.zeros_like(top)
    for p in parts:
        factor = jnp.exp(p[0:4] - top)
        total = total + p[4:8] * factor
        weighted = weighted + p[8:12] * factor
    return top, total, weighted


def kernel(
    tok_hbm,
    cot_hbm,
    cb_hbm,
    idx_hbm,
    grad_tok_ref,
    grad_cb_ref,
    tok_ref,
    cot_ref,
    cb_ref,
    idx_ref,
    load_sem,
    expo,
    back,
    direct,
    cbt,
    uv_own,
    uv_other,
    uv_send,
    uv_recv,
    stat_own,
    stat_other,
    stat_1,
    stat_2,
    mix,
    sum_2,
    final,
    cb_send,
    cb_recv,
    far_recv,
    cb_own,
    core_send,
    core_recv,
    ring_send,
    ring_recv,
    final_recv,
    x_send,
    x_recv,
):
    code = lax.axis_index("code")
    x = lax.axis_index("tok")
    y, z, core = code // 16, (code // 2) % 8, code % 2
    other = (code + 1 - 2 * core, x)
    x_size = 4

    def along(axis, k):
        if axis == "z":
            return (y * 16 + ((z + k) % RING) * 2 + core, x)
        return (((y + k) % RING) * 16 + z * 2 + core, x)

    first = (("z", z), ("y", y))
    second = (("y", y), ("z", z))

    loads = [
        pltpu.make_async_copy(src, dst, load_sem.at[i])
        for i, (src, dst) in enumerate(
            ((cb_hbm, cb_ref), (tok_hbm, tok_ref), (cot_hbm, cot_ref), (idx_hbm, idx_ref))
        )
    ]
    for load in loads:
        load.start()

    barrier = pltpu.get_barrier_semaphore()

    def greet(k, carry):
        for axis in ("z", "y"):
            pl.semaphore_signal(barrier, inc=1, device_id=along(axis, k), device_id_type=MESH)
        return carry

    lax.fori_loop(1, RING, greet, 0)
    for k in (1, x_size - 1):
        pl.semaphore_signal(barrier, inc=1, device_id=(code, (x + k) % x_size), device_id_type=MESH)
    pl.semaphore_signal(barrier, inc=1, device_id=other, device_id_type=MESH)

    def ring_copy(buf, stage, half, axis, me, k, src=None):
        return pltpu.make_async_remote_copy(
            src_ref=buf.at[half, me] if src is None else src.at[half, (me + k) % RING],
            dst_ref=buf.at[half, me],
            send_sem=ring_send.at[stage],
            recv_sem=ring_recv.at[stage],
            device_id=along(axis, k),
            device_id_type=MESH,
        )

    def ring_start(buf, stage, order, src=None, halves=(0, 1)):
        for k in FAR_FIRST:
            for half in halves:
                ring_copy(buf, stage, half, *order[half], k, src).start()

    def ring_bytes(buf, stage):
        blocks = buf.at[:, pl.ds(0, RING - 1)]
        return pltpu.make_async_remote_copy(
            src_ref=blocks,
            dst_ref=blocks,
            send_sem=ring_send.at[stage],
            recv_sem=ring_recv.at[stage],
            device_id=other,
            device_id_type=MESH,
        )

    def core_copy(src, dst, index):
        return pltpu.make_async_remote_copy(
            src_ref=src,
            dst_ref=dst,
            send_sem=core_send.at[index],
            recv_sem=core_recv.at[index],
            device_id=other,
            device_id_type=MESH,
        )

    def fold(value, op):
        return op(value.reshape(CODES // 8, 8, TOK), axis=0)

    loads[0].wait()
    loads[1].wait()
    logits = lax.dot_general(cb_ref[...], tok_ref[...], NT, preferred_element_type=F32)
    expo[...] = logits
    loads[2].wait()
    back[...] = lax.dot_general(cb_ref[...], cot_ref[...], NT, preferred_element_type=F32)
    top = jnp.max(fold(logits, jnp.max), axis=0, keepdims=True)
    e = jnp.exp(expo[...] - top)
    expo[...] = e
    total = jnp.sum(fold(e, jnp.sum), axis=0, keepdims=True)
    weighted = jnp.sum(fold(e * back[...], jnp.sum), axis=0, keepdims=True)

    for half in range(2):
        span = slice(half * HALF, (half + 1) * HALF)
        stat_own[half, 0:4] = to_grid(top[:, span])
        stat_own[half, 4:8] = to_grid(total[:, span])
        stat_own[half, 8:12] = to_grid(weighted[:, span])
    pl.semaphore_wait(barrier, 2 * (RING - 1) + 2 + 1)
    stat_copy = core_copy(stat_own, stat_other, 0)
    stat_copy.start()

    eye = lax.broadcasted_iota(jnp.int32, (D, D), 0) == lax.broadcasted_iota(jnp.int32, (D, D), 1)
    eye = jnp.where(eye, 1.0, 0.0).astype(BF16)
    cbt[...] = lax.dot_general(eye, cb_ref[...], NT, preferred_element_type=F32).astype(BF16)

    def v_terms(half):
        weight = expo[:, half * HALF : (half + 1) * HALF].astype(BF16)
        return jnp.dot(cbt[...], weight, preferred_element_type=F32)

    stat_copy.wait()

    scale, mean = [], []
    for half in range(2):
        states = [jnp.where(core == 0, a, b) for a, b in ((stat_own[half], stat_other[half]), (stat_other[half], stat_own[half]))]
        pair_top, pair_total, pair_weighted = combine(states)
        me = first[half][1]
        stat_1[half, me, 0:4] = pair_top
        stat_1[half, me, 4:8] = pair_total
        stat_1[half, me, 8:12] = pair_weighted
        scale.append(to_row(jnp.exp(stat_own[half, 0:4] - pair_top)))
        mean.append(to_row(pair_weighted / pair_total))
    ring_start(stat_1, 0, first)

    uv_copies = [
        [core_copy(uv_own.at[which, half, 1 - core], uv_other.at[which, half], 1 + 2 * which + half) for half in range(2)]
        for which in range(2)
    ]

    def uv_chip(which, half, value):
        for c in range(2):
            uv_own[which, half, c] = value[c * 128 : (c + 1) * 128].astype(BF16)
        uv_copies[which][half].start()

    def u_terms(half):
        span = slice(half * HALF, (half + 1) * HALF)
        weight = (expo[:, span] * scale[half] * (back[:, span] - mean[half])).astype(BF16)
        return jnp.dot(cbt[...], weight, preferred_element_type=F32)

    def uv_sum(which, half):
        uv_copies[which][half].wait()
        both = uv_own[which, half, core].astype(F32) + uv_other[which, half].astype(F32)
        for k in range(RING):
            uv_send[which, half, k] = both[k * ROWS : (k + 1) * ROWS].astype(BF16)
        uv_recv[which, half, first[half][1]] = uv_send[which, half, first[half][1]]

    uv_chip(1, 0, v_terms(0) * scale[0])
    uv_chip(1, 1, v_terms(1) * scale[1])
    uv_chip(0, 0, u_terms(0))
    uv_chip(0, 1, u_terms(1))
    uv_sum(1, 0)
    uv_sum(1, 1)
    ring_start(uv_recv.at[1], 1, first, uv_send.at[1])
    uv_sum(0, 0)

    ring_bytes(stat_1, 0).wait_recv()
    for half in range(2):
        ring_top, ring_total, ring_weighted = combine([stat_1[half, j] for j in range(RING)])
        me = second[half][1]
        stat_2[half, me, 0:4] = ring_top
        stat_2[half, me, 4:8] = ring_total
        stat_2[half, me, 8:12] = ring_weighted
    ring_start(stat_2, 2, second)
    ring_start(uv_recv.at[0], 5, first, uv_send.at[0], (0,))
    uv_sum(0, 1)
    ring_start(uv_recv.at[0], 5, first, uv_send.at[0], (1,))

    loads[3].wait()
    hot = lax.broadcasted_iota(jnp.int32, (CODES, TOK), 0) == idx_ref[...] - code * CODES
    hot = jnp.where(hot, 1.0, 0.0).astype(BF16)
    direct[...] = jnp.dot(hot, cot_ref[...], preferred_element_type=F32)

    ring_bytes(stat_2, 2).wait_recv()
    state = [combine([stat_2[half, j] for j in range(RING)]) for half in range(2)]
    ratio = [w / t for _, t, w in state]
    local_scale = jnp.concatenate(
        [to_row(jnp.exp(stat_own[half, 0:4] - state[half][0]) / state[half][1]) for half in range(2)], axis=1
    )
    ratio_row = jnp.concatenate([to_row(ratio[half]) for half in range(2)], axis=1)

    low, high = pl.ds(0, QUARTER // 2), pl.ds(QUARTER // 2, QUARTER // 2)

    def x_copy(src, dst, send, recv, side):
        return pltpu.make_async_remote_copy(
            src_ref=src,
            dst_ref=dst,
            send_sem=x_send.at[send],
            recv_sem=x_recv.at[recv],
            device_id=(code, (x + (1, x_size - 1)[side]) % x_size),
            device_id_type=MESH,
        )

    far_copies = [x_copy(cb_send.at[2, part], far_recv.at[side], 0, side, side) for side, part in ((0, low), (1, high))]
    near_copies = [
        x_copy(cb_send.at[side, part], cb_recv.at[side, part], 1, 2, side) for side, part in ((0, high), (1, low))
    ]
    sum_copies = [
        x_copy(cb_send.at[side, part], cb_recv.at[side, part], 1, 2, side) for side, part in ((0, low), (1, high))
    ]

    def code_rows(k):
        rows = pl.ds(pl.multiple_of(((x + k) % x_size) * QUARTER, QUARTER), QUARTER)
        grad = (expo[rows] * local_scale * (back[rows] - ratio_row)).astype(BF16)
        return jnp.dot(grad, tok_ref[...], preferred_element_type=F32) + direct[rows]

    for half in range(2):
        for j in range(RING):
            peer = stat_1[half, j]
            factor = jnp.exp(peer[0:4] - state[half][0]) / state[half][1]
            shift = peer[8:12] / peer[4:8] - ratio[half]
            mix[half, j, 0:1] = to_row(factor)
            mix[half, j, 1:2] = to_row(factor * shift)
    ring_bytes(uv_recv.at[1], 1).wait_recv()
    ring_bytes(uv_recv.at[0], 5).wait_recv()
    for half in range(2):
        acc = jnp.zeros((ROWS, HALF), F32)
        for j in range(RING):
            acc = acc + mix[half, j, 0:1] * uv_recv[0, half, j].astype(F32)
            acc = acc + mix[half, j, 1:2] * uv_recv[1, half, j].astype(F32)
        sum_2[half, second[half][1]] = acc.astype(BF16)
    ring_start(sum_2, 3, second)

    cb_send[2] = code_rows(2).astype(BF16)
    for copy in far_copies:
        copy.start()


    mid = QUARTER // 2
    part = code_rows(1)
    cb_send[0, high] = part[mid:].astype(BF16)
    near_copies[0].start()
    cb_own[0] = part[:mid]
    part = code_rows(3)
    cb_send[1, low] = part[:mid].astype(BF16)
    near_copies[1].start()
    cb_own[1] = part[mid:]
    grad_cb_ref[...] = code_rows(0)

    ring_bytes(sum_2, 3).wait_recv()
    for half in range(2):
        acc = functools.reduce(jnp.add, [sum_2[half, j].astype(F32) for j in range(RING)])
        final[core, half, first[half][1]] = acc.astype(BF16)

    def final_copy(half, k, slot):
        axis, me = first[half]
        return pltpu.make_async_remote_copy(
            src_ref=final.at[core, half, slot],
            dst_ref=final.at[core, half, slot],
            send_sem=ring_send.at[4],
            recv_sem=final_recv.at[k],
            device_id=along(axis, k),
            device_id_type=MESH,
        )

    def final_forward(half, slot):
        return core_copy(final.at[core, half, slot], final.at[core, half, slot], 5)

    for k in FAR_FIRST:
        for half in range(2):
            final_copy(half, k, first[half][1]).start()
    for half in range(2):
        final_forward(half, first[half][1]).start()
    for side, part in ((0, low), (1, high)):
        far_copies[side].wait_recv()
        cb_send[side, part] = (cb_own[side] + far_recv[side].astype(F32)).astype(BF16)
        sum_copies[side].start()
    for k in reversed(FAR_FIRST):
        both = final.at[core, :, 0]
        pltpu.make_async_remote_copy(
            src_ref=both,
            dst_ref=both,
            send_sem=ring_send.at[4],
            recv_sem=final_recv.at[RING - k],
            device_id=other,
            device_id_type=MESH,
        ).wait_recv()
        for half in range(2):
            final_forward(half, (first[half][1] + k) % RING).start()

    def turn_rows(c):
        for half in range(2):
            block = jnp.concatenate([final[c, half, j].astype(F32) for j in range(RING)], axis=0)
            lanes = pl.ds(pl.multiple_of(c * 128, 128), 128)
            grad_tok_ref[half * HALF : (half + 1) * HALF, lanes] = block.T

    turn_rows(core)
    x_copy(cb_send.at[pl.ds(0, 2)], cb_recv, 1, 2, 0).wait_recv()
    grad_cb_ref[...] += cb_recv[0].astype(F32) + cb_recv[1].astype(F32)
    core_copy(final.at[core], final.at[1 - core], 5).wait()
    turn_rows(1 - core)

    ring_bytes(stat_1, 0).wait_send()
    ring_bytes(uv_send.at[1], 1).wait_send()
    ring_bytes(uv_send.at[0], 5).wait_send()
    ring_bytes(stat_2, 2).wait_send()
    ring_bytes(sum_2, 3).wait_send()

    ring_bytes(final.at[core], 4).wait_send()
    x_copy(cb_send.at[2], cb_send.at[2], 0, 0, 0).wait_send()
    x_copy(cb_send.at[pl.ds(0, 2)], cb_recv, 1, 2, 0).wait_send()


def write(grad_tok_ref, grad_cb_ref, tok_out, cb_out, sems):
    copies = [
        pltpu.make_async_copy(grad_tok_ref, tok_out, sems.at[0]),
        pltpu.make_async_copy(grad_cb_ref, cb_out, sems.at[1]),
    ]
    for copy in copies:
        copy.start()
    for copy in copies:
        copy.wait()


def shards(tokens, codebook, cotangent, indices):
    vmem = pl.BlockSpec(memory_space=pltpu.VMEM)
    hbm = pl.BlockSpec(memory_space=pltpu.HBM)
    shapes = (
        jax.ShapeDtypeStruct((TOK, D), F32),
        jax.ShapeDtypeStruct((QUARTER, D), F32),
    )
    grads = pl.pallas_call(
        kernel,
        out_shape=shapes,
        in_specs=[hbm] * 4,
        out_specs=(vmem, vmem),
        scratch_shapes=[
            pltpu.VMEM((TOK, D), BF16),
            pltpu.VMEM((TOK, D), BF16),
            pltpu.VMEM((CODES, D), BF16),
            pltpu.VMEM((1, TOK), jnp.int32),
            pltpu.SemaphoreType.DMA((4,)),
            pltpu.VMEM((CODES, TOK), F32),
            pltpu.VMEM((CODES, TOK), F32),
            pltpu.VMEM((CODES, D), F32),
            pltpu.VMEM((D, CODES), BF16),
            pltpu.VMEM((2, 2, 2, 128, HALF), BF16),
            pltpu.VMEM((2, 2, 128, HALF), BF16),
            pltpu.VMEM((2, 2, RING, ROWS, HALF), BF16),
            pltpu.VMEM((2, 2, RING, ROWS, HALF), BF16),
            pltpu.VMEM((2, 12, 128), F32),
            pltpu.VMEM((2, 12, 128), F32),
            pltpu.VMEM((2, RING, 12, 128), F32),
            pltpu.VMEM((2, RING, 12, 128), F32),
            pltpu.VMEM((2, RING, 2, HALF), F32),
            pltpu.VMEM((2, RING, ROWS, HALF), BF16),
            pltpu.VMEM((2, 2, RING, ROWS, HALF), BF16),
            pltpu.VMEM((3, QUARTER, D), BF16),
            pltpu.VMEM((2, QUARTER, D), BF16),
            pltpu.VMEM((2, QUARTER // 2, D), BF16),
            pltpu.VMEM((2, QUARTER // 2, D), F32),
            pltpu.SemaphoreType.DMA((6,)),
            pltpu.SemaphoreType.DMA((6,)),
            pltpu.SemaphoreType.DMA((6,)),
            pltpu.SemaphoreType.DMA((6,)),
            pltpu.SemaphoreType.DMA((RING,)),
            pltpu.SemaphoreType.DMA((2,)),
            pltpu.SemaphoreType.DMA((3,)),
        ],
        compiler_params=pltpu.CompilerParams(
            collective_id=0, has_side_effects=True, vmem_limit_bytes=VMEM_LIMIT
        ),
        name="quantizer_backward",
    )(*(pltpu.with_memory_space_constraint(a, pltpu.HBM) for a in (tokens, cotangent, codebook, indices.reshape(1, TOK))))
    return pl.pallas_call(
        write,
        out_shape=shapes,
        in_specs=[vmem, vmem],
        out_specs=(hbm, hbm),
        scratch_shapes=[pltpu.SemaphoreType.DMA((2,))],
        compiler_params=pltpu.CompilerParams(vmem_limit_bytes=8 * 1024 * 1024),
        name="write_out",
    )(*grads)


def solution(mesh):
    return jax.shard_map(
        shards,
        mesh=mesh,
        in_specs=(P("tok", None), P("code", None), P("tok", None), P("tok")),
        out_specs=(P("tok", None), P(("code", "tok"), None)),
        check_vma=False,
    )
```
